512 devices in a mesh: tm: 32 (over z, core), seq: 16 (over x, y).
Axes of the slice: x: 4, y: 4, z: 16, core: 2. Of those that a mesh axis runs over, the one named last changes fastest.
Arguments:
- states: float32 [32, 512, 64], P('tm', 'seq'), may hold values from -6 to 6
- initial: float32 [512, 64], P('seq'), may hold values from -6 to 6
- noise_draws: float32 [32, 512, 64], P('tm', 'seq'), may hold values from -6 to 6
- timesteps: int32 [32, 2], P('tm'), may hold values from 0 to 999, as said below
- context: bfloat16 [512, 5120], P('seq'), may hold values from -6 to 6
- modulation: float32 [32, 2, 5120], P('tm'), may hold values from -1.5 to 1.5
- out_gate: float32 [32, 64], P('tm'), may hold values from -3 to 3
- embed_weight: bfloat16 [64, 5120], replicated, may hold values from -0.75 to 0.75
- qkv_weight: bfloat16 [3, 5120, 4096], P(None, 'tm', 'seq'), may hold values from -1 to 1
- out_weight: bfloat16 [4096, 5120], P('seq', 'tm'), may hold values from -0.09375 to 0.09375
- head_weight: bfloat16 [64, 5120], P(None, 'tm'), may hold values from -0.078125 to 0.078125
Outputs:
- new_states: float32 [32, 512, 64], P('tm', 'seq')
- velocity: bfloat16 [32, 512, 64], P('tm', 'seq')
The draws below stay inside these ranges and needn't reach their ends.
Inputs may be any that keep to these rules, and one draw needn't show every extreme that they name: `timesteps`: row k holds step k's timestep index and the next, smaller one, which is the first entry of row k + 1; row 0 starts at 999.
All inputs are finite; a program needn't handle non-finite values.
Results may differ from the reference program's by a relative error of at most 0.02.
Values may be sent and summed in bfloat16 or wider, within the bound.
No kernel may reach another device: no remote copies, remote signals or barrier semaphores. Data moves between devices by JAX's collectives and lax.ppermute only.
A program may use at most 64 MiB of HBM per device.

```python
import math
import jax
import jax.numpy as jnp
from jax import lax

C = 64
D = 5120
HEAD = 128
NT = 1000
HEADS = 32
TOKENS = 512
STEPS = 32


def draw_timesteps(key, part):
    key = jax.random.fold_in(key, 11)
    top_gap = (NT - 1) // STEPS + 1
    low_gap = max(1, top_gap // 2)
    spacing = jax.random.randint(key, (STEPS,), low_gap, top_gap)
    levels = NT - 1 - jnp.concatenate([jnp.zeros((1,), jnp.int32), jnp.cumsum(spacing).astype(jnp.int32)])
    return jnp.stack([levels[:-1], levels[1:]], axis=1).astype(jnp.int32)


def draw_states(key, part):
    key = jax.random.fold_in(key, 12)
    values = jax.random.normal(key, (STEPS, TOKENS, C))
    return jnp.clip(values, -6.0, 6.0).astype(jnp.float32)


def draw_context(key, part):
    key = jax.random.fold_in(key, 14)
    values = jax.random.normal(key, (TOKENS, D))
    return jnp.clip(values, -6.0, 6.0).astype(jnp.bfloat16)


def draw_qkv_weight(key, part):
    key = jax.random.fold_in(key, 13)
    sub_keys = jax.random.split(key, 1)
    base = jax.random.normal(sub_keys[0], (3, D, HEADS, HEAD))
    scales = jnp.array([1.3, 1.3, 1.0], jnp.float32).reshape(3, 1, 1, 1) / math.sqrt(D)
    return jnp.clip(base * scales, -1.0, 1.0).reshape(3, D, HEADS * HEAD).astype(jnp.bfloat16)


def block_scale(key, shape, shards, low, top_value):
    gain = 1.0
    for axis_at, blocks in shards:
        steps = jax.random.uniform(jax.random.fold_in(jax.random.fold_in(key, 6), axis_at), (blocks,), jnp.float32, low / len(shards), top_value / len(shards))
        gain = gain * jnp.repeat(jnp.exp(steps), shape[axis_at] // blocks).reshape((-1,) + (1,) * (len(shape) - 1 - axis_at))
    return gain


def bell_draw(key, dims, scale, most, shards=(), dtype=jnp.bfloat16):
    values = scale * jax.random.normal(key, dims, jnp.float32)
    if shards:
        values = values * block_scale(key, dims, shards, -0.22, 0.18)
    return jnp.clip(values, -most, most).astype(dtype)


def setup_inputs(seed: int = 0) -> dict:
    splits = jax.random.split(jax.random.key(seed), 12)
    states = draw_states(jax.random.fold_in(splits[11], 71), 0)
    initial = bell_draw(splits[1], (TOKENS, C), 1.0, 6.0, ((0, 16),), jnp.float32)
    noise_draws = bell_draw(splits[2], (STEPS, TOKENS, C), 1.0, 6.0, ((0, 32), (1, 16)), jnp.float32)
    timesteps = draw_timesteps(jax.random.fold_in(splits[11], 71), 0)
    context = draw_context(jax.random.fold_in(splits[11], 71), 0)
    modulation = bell_draw(splits[5], (STEPS, 2, D), 0.3, 1.5, ((0, 32),), jnp.float32)
    out_gate = bell_draw(splits[6], (STEPS, C), 0.5, 3.0, ((0, 32),), jnp.float32)
    embed_weight = bell_draw(splits[7], (C, D), C ** -0.5, 0.75)
    qkv_weight = draw_qkv_weight(jax.random.fold_in(splits[11], 71), 0)
    out_weight = bell_draw(splits[9], (HEADS * HEAD, D), (HEADS * HEAD) ** -0.5, 0.09375, ((0, 16), (1, 32)))
    head_weight = bell_draw(splits[10], (C, D), D ** -0.5, 0.078125, ((1, 32),))
    return dict(states=states, initial=initial, noise_draws=noise_draws, timesteps=timesteps, context=context, modulation=modulation, out_gate=out_gate, embed_weight=embed_weight, qkv_weight=qkv_weight, out_weight=out_weight, head_weight=head_weight)


def sigma_of(level_ids):
    fraction = (level_ids.astype(jnp.float32) + 1.0) / NT
    return 5.0 * fraction / (1.0 + 4.0 * fraction)

def attend_block(query_block, keys_all, values_all):
    scores = jnp.einsum('qhd,khd->hqk', query_block.astype(jnp.float32), keys_all.astype(jnp.float32)) / math.sqrt(query_block.shape[-1])
    row_peak = lax.optimization_barrier(jnp.max(scores, axis=-1, keepdims=True))
    weights = jnp.exp(scores - row_peak)
    probs = weights / lax.optimization_barrier(jnp.sum(weights, axis=-1, keepdims=True))
    probs_bf = probs.astype(jnp.bfloat16)
    output = jnp.einsum('hqk,khd->qhd', probs_bf.astype(jnp.float32), values_all.astype(jnp.float32))
    return output.astype(jnp.bfloat16)

def step_velocity(current, mods, gate_row, context, embed_weight, qkv_weight, out_weight, head_weight):
    latent_bf = current.astype(jnp.bfloat16)
    hidden = jnp.dot(latent_bf, embed_weight, preferred_element_type=jnp.float32) + context.astype(jnp.float32)
    mean_square = lax.optimization_barrier(jnp.mean(hidden * hidden, axis=-1, keepdims=True))
    normed = hidden * lax.rsqrt(mean_square + 1e-06)
    modded = (normed * (1.0 + mods[1]) + mods[0]).astype(jnp.bfloat16)
    queries = jnp.dot(modded, qkv_weight[0], preferred_element_type=jnp.float32).astype(jnp.bfloat16).reshape(TOKENS, HEADS, HEAD)
    keys_all = jnp.dot(modded, qkv_weight[1], preferred_element_type=jnp.float32).astype(jnp.bfloat16).reshape(TOKENS, HEADS, HEAD)
    values_all = jnp.dot(modded, qkv_weight[2], preferred_element_type=jnp.float32).astype(jnp.bfloat16).reshape(TOKENS, HEADS, HEAD)
    block_rows = min(512, TOKENS)
    blocks = queries.reshape(TOKENS // block_rows, block_rows, HEADS, HEAD)

    def one_block(query_block):
        return attend_block(query_block, keys_all, values_all)
    attended = lax.map(one_block, blocks).reshape(TOKENS, HEADS * HEAD)
    mixed = jnp.dot(attended, out_weight, preferred_element_type=jnp.float32)
    readout = jnp.dot(mixed, head_weight.astype(jnp.float32).T, precision=lax.Precision.HIGHEST)
    return (1.0 + gate_row) * readout

def reference(states, initial, noise_draws, timesteps, context, modulation, out_gate, embed_weight, qkv_weight, out_weight, head_weight):

    def one_step(group):
        return step_velocity(group[0], group[1], group[2], context, embed_weight, qkv_weight, out_weight, head_weight)
    velocity_f = lax.map(one_step, (states, modulation, out_gate))
    step_size = (sigma_of(timesteps[:, 1]) - sigma_of(timesteps[:, 0]))[:, None, None]
    drift_term = step_size * velocity_f + jnp.sqrt(-step_size) * noise_draws
    running = jnp.cumsum(drift_term, axis=0)[:-1]
    before = jnp.concatenate([jnp.zeros((1, TOKENS, C), jnp.float32), running], axis=0)
    new_states = initial[None] + before
    return (new_states, velocity_f.astype(jnp.bfloat16))
```

```python
import functools
import math

import jax
import jax.numpy as jnp
from jax import lax
from jax.experimental import pallas as pl
from jax.experimental.pallas import tpu as pltpu
from jax.sharding import PartitionSpec as P

HEAD = 128
NT = 1000
F32 = jnp.float32
BF16 = jnp.bfloat16
VMEM_LIMIT = 56 * 1024 * 1024
GROUPS = (10, 3, 3)


def sigma_of(level_ids):
    fraction = (level_ids.astype(F32) + 1.0) / NT
    return 5.0 * fraction / (1.0 + 4.0 * fraction)


def dot_nt(a, b):
    return lax.dot_general(a, b, (((1,), (1,)), ((), ())), preferred_element_type=F32)


def dot_nn(a, b):
    return lax.dot_general(a, b, (((1,), (0,)), ((), ())), preferred_element_type=F32)


def split_two(value):
    high = value.astype(BF16)
    return high, (value - high.astype(F32)).astype(BF16)


def kernel_call(body, out_shape, n_in, n_smem=0, flops=0, moved=0, aliases=None):
    one = pl.BlockSpec(memory_space=pltpu.VMEM)
    scalar = pl.BlockSpec(memory_space=pltpu.SMEM)
    many = isinstance(out_shape, (tuple, list))
    return pl.pallas_call(
        body,
        out_shape=out_shape,
        in_specs=[scalar] * n_smem + [one] * n_in,
        out_specs=[one] * len(out_shape) if many else one,
        input_output_aliases=aliases or {},
        compiler_params=pltpu.CompilerParams(vmem_limit_bytes=VMEM_LIMIT),
        cost_estimate=pl.CostEstimate(flops=flops, bytes_accessed=moved, transcendentals=0),
    )


def pack_weights(qkv_ref, out_ref, head_ref, chunk_ref):
    count, rows, _ = qkv_ref.shape
    for i in range(count):
        chunk_ref[i * rows : (i + 1) * rows, :] = qkv_ref[i]
    chunk_ref[count * rows :, :] = dot_nt(head_ref[...], out_ref[...]).astype(BF16)


def pack_context(core_ref, states_ref, embed_ref, context_ref, mods_ref, payload_ref, embed_out, mine_ref, other_ref):
    chips, _, rows = embed_out.shape
    peers = payload_ref.shape[0]
    tokens, width = context_ref.shape
    channels = embed_ref.shape[0]
    second = core_ref[0] == 1
    latent = states_ref[...].astype(BF16)
    context = context_ref[...].astype(F32)
    hidden = dot_nn(latent, embed_ref[...]) + context
    scale = lax.rsqrt(jnp.mean(hidden * hidden, axis=-1, keepdims=True) + 1e-06)

    def halves(value):
        moved = pltpu.roll(value, width - rows, 1)
        return jnp.where(second, moved, value), jnp.where(second, value, moved)

    mine, _ = halves(context)
    for j in range(chips):
        payload_ref[0, :, j * rows : (j + 1) * rows] = mine[:, 2 * j * rows : (2 * j + 1) * rows].astype(BF16)
    high, low = split_two(scale)
    base = chips * rows
    lane = lax.broadcasted_iota(jnp.int32, (tokens, 128), 1)
    tail = jnp.concatenate([latent.astype(F32), jnp.zeros((tokens, 128 - channels), F32)], axis=1)
    tail = jnp.where(lane == channels, high.astype(F32), tail)
    tail = jnp.where(lane == channels + 1, low.astype(F32), tail)
    payload_ref[0, :, base:] = tail.astype(BF16)
    for p in range(1, peers):
        payload_ref[p] = payload_ref[0]
    mine, _ = halves(embed_ref[...].astype(F32))
    for j in range(chips):
        embed_out[j] = mine[:, 2 * j * rows : (2 * j + 1) * rows].astype(BF16)
    mine, other = halves(mods_ref[...])
    for j in range(chips):
        mine_ref[j] = mine[:, 2 * j * rows : (2 * j + 1) * rows]
        other_ref[j] = other[:, 2 * j * rows : (2 * j + 1) * rows]


def cut_context(full_ref, blocks_ref, tail_ref):
    chips, _, rows = blocks_ref.shape
    for j in range(chips):
        blocks_ref[j] = full_ref[:, j * rows : (j + 1) * rows]
    tail_ref[...] = full_ref[:, chips * rows :]


def project(chunk_count, first, last, *refs):
    where_ref, blocks_ref, embed_ref, mine_ref, other_ref = refs[:5]
    chunk_refs = refs[5 : 5 + chunk_count]
    refs = refs[5 + chunk_count :]
    if not first:
        sums_ref, heads_ref = refs[:2]
        refs = refs[2:]
    rows = blocks_ref.shape[2]
    half = blocks_ref.shape[1] + embed_ref.shape[1] + 16
    count = 3
    total = [None] * count
    heads = None if first else heads_ref[...]
    for at, chunk_ref in enumerate(chunk_refs):
        chip = where_ref[at]
        context = blocks_ref[chip].astype(F32)
        embed = embed_ref[chip].astype(F32)
        parts = []
        for mods_ref in (mine_ref, other_ref):
            mods = mods_ref[chip]
            gain = 1.0 + mods[1:2]
            parts.append((context * gain).astype(BF16))
            parts.append((embed * gain).astype(BF16))
            row = lax.broadcasted_iota(jnp.int32, (16, rows), 0)
            parts.append(jnp.where(row == 0, mods[0:1], 0.0).astype(BF16))
        left = jnp.concatenate(parts, axis=0)
        for i in range(count):
            term = dot_nn(left, chunk_ref[i * rows : (i + 1) * rows, :])
            total[i] = term if total[i] is None else total[i] + term
        share = chunk_ref[count * rows :, :].astype(F32)
        heads = share if heads is None else heads + share
    if not first:
        total = [total[i] + sums_ref[i] for i in range(count)]
    if last:
        own_ref, send_ref = refs
        for i in range(count):
            own_ref[i * half : (i + 1) * half, :] = total[i][:half]
            send_ref[i * half : (i + 1) * half, :] = total[i][half:].astype(BF16)
        own_ref[count * half :, :] = heads
        send_ref[count * half :, :] = heads.astype(BF16)
    else:
        sums_out, heads_out = refs
        for i in range(count):
            sums_out[i] = total[i]
        heads_out[...] = heads


def attend(own_ref, got_ref, tail_ref, out_ref):
    peers, pair_rows, lanes = out_ref.shape
    channels = lanes // 2
    tokens = tail_ref.shape[0]
    half = tokens + channels + 16
    latent = tail_ref[:, :channels]
    scale = tail_ref[:, channels : channels + 1].astype(F32) + tail_ref[:, channels + 1 : channels + 2].astype(F32)
    made = []
    for i in range(3):
        at = i * half
        body = own_ref[at : at + tokens, :] + got_ref[at : at + tokens, :].astype(F32)
        at += tokens
        embed = own_ref[at : at + channels, :] + got_ref[at : at + channels, :].astype(F32)
        at += channels
        shift = own_ref[at : at + 16, :] + got_ref[at : at + 16, :].astype(F32)
        high, low = split_two(embed)
        body = body + dot_nn(latent, high) + dot_nn(latent, low)
        made.append((body * scale + shift[0:1]).astype(BF16))
    queries, keys, values = made
    outs = []
    for h in range(queries.shape[1] // HEAD):
        cols = slice(h * HEAD, (h + 1) * HEAD)
        scores = dot_nt(queries[:, cols], keys[:, cols]) * (1.0 / math.sqrt(HEAD))
        weights = jnp.exp(scores - jnp.max(scores, axis=-1, keepdims=True))
        total = jnp.sum(weights, axis=-1, keepdims=True)
        outs.append((dot_nn(weights.astype(BF16), values[:, cols]) / total).astype(BF16))
    attended = jnp.concatenate(outs, axis=1)
    heads = own_ref[3 * half :, :] + got_ref[3 * half :, :].astype(F32)
    high, low = split_two(heads)
    result = dot_nt(attended, high) + dot_nt(attended, low)
    for p in range(peers):
        at = 2 * p * pair_rows
        block = jnp.concatenate([result[at : at + pair_rows], result[at + pair_rows : at + 2 * pair_rows]], axis=1)
        out_ref[p] = block.astype(BF16)


def per_device(
    states, initial, noise_draws, timesteps, context, modulation, out_gate, embed_weight, qkv_weight, out_weight, head_weight
):
    steps, peers = lax.axis_size("tm"), lax.axis_size("seq")
    chips = steps // 2
    mine = lax.axis_index("tm")
    z, core = mine // 2, mine % 2
    tokens_here, channels = initial.shape
    width = context.shape[1]
    rows = qkv_weight.shape[1]
    cols = qkv_weight.shape[2]
    tokens = tokens_here * peers
    half = tokens + channels + 16
    shape = jax.ShapeDtypeStruct

    flip = [(i, i ^ 1) for i in range(steps)]
    forth = [(i, (i + (2 if i % 2 == 0 else -2)) % steps) for i in range(steps)]
    back = [(b, a) for a, b in forth]

    payload, embed_blocks, mods_mine, mods_other = kernel_call(
        pack_context,
        (
            shape((peers, tokens_here, chips * rows + 128), BF16),
            shape((chips, channels, rows), BF16),
            shape((chips, 2, rows), F32),
            shape((chips, 2, rows), F32),
        ),
        4,
        1,
        flops=2 * tokens_here * channels * width,
        moved=5000000,
    )(core[None], states[0], embed_weight, context, modulation[0])
    gathered = lax.all_to_all(payload, "seq", 0, 0).reshape(tokens, chips * rows + 128)

    chunk = kernel_call(
        pack_weights, shape((3 * rows + channels, cols), BF16), 3, flops=2 * channels * rows * cols, moved=700000
    )(qkv_weight, out_weight, head_weight)
    mods_sibling = lax.ppermute(mods_other, "tm", flip)

    sign = 1 - 2 * core
    arrived, places = [chunk], [z]
    ahead = behind = chunk
    for k in range(1, chips // 2 + 1):
        ahead = lax.ppermute(ahead, "tm", forth)
        arrived.append(ahead)
        places.append((z - sign * k) % chips)
        if k < chips // 2:
            behind = lax.ppermute(behind, "tm", back)
            arrived.append(behind)
            places.append((z + sign * k) % chips)
    places = jnp.stack(places).astype(jnp.int32)

    blocks, tail = kernel_call(
        cut_context, (shape((chips, tokens, rows), BF16), shape((tokens, 128), BF16)), 1, moved=8000000
    )(gathered)

    groups = GROUPS if sum(GROUPS) == len(arrived) else (len(arrived) - 1, 1)
    at, sums = 0, ()
    for g, size in enumerate(groups):
        first, last = g == 0, g == len(groups) - 1
        if last:
            out_shape = (shape((3 * half + channels, cols), F32), shape((3 * half + channels, cols), BF16))
        else:
            out_shape = (shape((3, 2 * half, cols), F32), shape((channels, cols), F32))
        sums = kernel_call(
            functools.partial(project, size, first, last),
            out_shape,
            4 + size + len(sums),
            1,
            flops=size * 2 * 2 * half * rows * 3 * cols,
            moved=8000000,
        )(places[at : at + size], blocks, embed_blocks, mods_mine, mods_sibling, *arrived[at : at + size], *sums)
        at += size
    own, send = sums
    got = lax.ppermute(send, "tm", flip)

    pair_rows = tokens_here // 2
    shares = kernel_call(
        attend, shape((peers, pair_rows, 2 * channels), BF16), 3, flops=600000000, moved=4000000
    )(own, got, tail)
    shares = lax.all_to_all(shares, "seq", 0, 0)
    mixed = jnp.sum(shares.astype(F32), axis=0)

    def pairs(value):
        return jnp.concatenate([value[:pair_rows], value[pair_rows:]], axis=1)

    def unpairs(value):
        return jnp.concatenate([value[:, :channels], value[:, channels:]], axis=0)

    gate = jnp.concatenate([out_gate, out_gate], axis=1)
    velocity_f = (1.0 + gate) * mixed
    step_size = sigma_of(timesteps[0, 1]) - sigma_of(timesteps[0, 0])
    drift = step_size * velocity_f + jnp.sqrt(-step_size) * pairs(noise_draws[0])
    both = lax.all_gather(drift, "tm", axis_index_groups=[[2 * i, 2 * i + 1] for i in range(chips)])
    same_core = [list(range(0, steps, 2)), list(range(1, steps, 2))]
    spread = jnp.broadcast_to((both[0] + both[1])[None], (chips, pair_rows, 2 * channels))
    everyone = lax.all_to_all(spread, "tm", 0, 0, axis_index_groups=same_core)
    earlier = lax.broadcasted_iota(jnp.int32, (chips, 1, 1), 0) < z
    before = jnp.sum(jnp.where(earlier, everyone, 0.0), axis=0) + jnp.where(core == 1, both[0], 0.0)
    new_states = initial + unpairs(before)
    return (new_states[None], unpairs(velocity_f).astype(BF16)[None])


def solution(mesh):
    in_specs = (
        P("tm", "seq", None),
        P("seq", None),
        P("tm", "seq", None),
        P("tm", None),
        P("seq", None),
        P("tm", None, None),
        P("tm", None),
        P(),
        P(None, "tm", "seq"),
        P("seq", "tm"),
        P(None, "tm"),
    )
    out_specs = (P("tm", "seq", None), P("tm", "seq", None))
    return jax.shard_map(per_device, mesh=mesh, in_specs=in_specs, out_specs=out_specs, check_vma=False)
```

```python
import functools
import math

import jax
import jax.numpy as jnp
from jax import lax
from jax.experimental import pallas as pl
from jax.experimental.pallas import tpu as pltpu
from jax.sharding import PartitionSpec as P

HEAD = 128
NT = 1000
F32 = jnp.float32
BF16 = jnp.bfloat16
KEPT = 14.0


def sigma_of(level_ids):
    fraction = (level_ids.astype(F32) + 1.0) / NT
    return 5.0 * fraction / (1.0 + 4.0 * fraction)


def dot_nt(a, b):
    return lax.dot_general(a, b, (((1,), (1,)), ((), ())), preferred_element_type=F32)


def dot_nn(a, b):
    return lax.dot_general(a, b, (((1,), (0,)), ((), ())), preferred_element_type=F32)


def split_two(value):
    high = value.astype(BF16)
    return high, (value - high.astype(F32)).astype(BF16)


def kernel_call(body, out_shape, n_in, n_smem=0, flops=0, moved=0, limit=24):
    one = pl.BlockSpec(memory_space=pltpu.VMEM)
    scalar = pl.BlockSpec(memory_space=pltpu.SMEM)
    many = isinstance(out_shape, (tuple, list))
    return pl.pallas_call(
        body,
        out_shape=out_shape,
        in_specs=[scalar] * n_smem + [one] * n_in,
        out_specs=[one] * len(out_shape) if many else one,
        compiler_params=pltpu.CompilerParams(vmem_limit_bytes=limit * 1024 * 1024),
        cost_estimate=pl.CostEstimate(flops=flops, bytes_accessed=moved, transcendentals=0),
    )


def pack_weights(qkv_ref, out_ref, head_ref, chunk_ref, share_ref):
    count, rows, cols = qkv_ref.shape
    row = lax.broadcasted_iota(jnp.int32, (16, cols), 0)
    meta = jnp.zeros((16, cols), F32)
    for i in range(count):
        weight = qkv_ref[i].astype(F32)
        peak = jnp.maximum(jnp.max(jnp.abs(weight), axis=0, keepdims=True), 1e-30)
        power = jnp.floor(-jnp.log2(peak))
        whole = jnp.round(weight * jnp.exp2(power + KEPT))
        chunk_ref[i * rows : (i + 1) * rows, :] = whole.astype(jnp.int32).astype(jnp.int16)
        meta = jnp.where(row == i, power, meta)
    chunk_ref[count * rows :, :] = meta.astype(jnp.int32).astype(jnp.int16)
    share_ref[...] = dot_nt(head_ref[...], out_ref[...]).astype(BF16)


def pack_context(rows, core_ref, states_ref, embed_ref, context_ref, mods_ref, payload_ref, embed_out, mine_ref, other_ref):
    peers, tokens, _ = payload_ref.shape
    channels, width = embed_ref.shape
    half = embed_out.shape[1]
    chips = half // rows
    second = core_ref[0] == 1
    latent = states_ref[...].astype(BF16)
    context = context_ref[...].astype(F32)

    def halves(value):
        moved = pltpu.roll(value, width - rows, 1)
        return jnp.where(second, moved, value), jnp.where(second, value, moved)

    def blocks(value, put):
        for j in range(chips):
            put(slice(j * rows, (j + 1) * rows), value[:, 2 * j * rows : (2 * j + 1) * rows])

    def put_context(at, value):
        payload_ref[0, :, at] = value.astype(BF16)

    def put_embed(at, value):
        embed_out[:, at] = value.astype(BF16)

    def put_mine(at, value):
        mine_ref[:, at] = value

    def put_other(at, value):
        other_ref[:, at] = value

    blocks(halves(context)[0], put_context)
    hidden = dot_nn(latent, embed_ref[...]) + context
    scale = lax.rsqrt(jnp.mean(hidden * hidden, axis=-1, keepdims=True) + 1e-06)
    high, low = split_two(scale)
    lane = lax.broadcasted_iota(jnp.int32, (tokens, 128), 1)
    tail = jnp.concatenate([latent.astype(F32), jnp.zeros((tokens, 128 - channels), F32)], axis=1)
    tail = jnp.where(lane == channels, high.astype(F32), tail)
    tail = jnp.where(lane == channels + 1, low.astype(F32), tail)
    payload_ref[0, :, half:] = tail.astype(BF16)
    for p in range(1, peers):
        payload_ref[p] = payload_ref[0]
    blocks(halves(embed_ref[...].astype(F32))[0], put_embed)
    mine, other = halves(mods_ref[...])
    blocks(mine, put_mine)
    blocks(other, put_other)


def project(rows, context_ref, embed_ref, mine_ref, other_ref, chunk_ref, own_ref, send_ref, sums_ref):
    at = pl.program_id(0)
    group = chunk_ref.shape[0]
    count, double, _ = sums_ref.shape
    half = double // 2
    context = context_ref[...].astype(F32)
    embed = embed_ref[...].astype(F32)
    row = lax.broadcasted_iota(jnp.int32, (16, group * rows), 0)
    parts = []
    for mods_ref in (mine_ref, other_ref):
        gain = 1.0 + mods_ref[1:2, :]
        parts.append((context * gain).astype(BF16))
        parts.append((embed * gain).astype(BF16))
        parts.append(jnp.where(row == 0, mods_ref[0:1, :], 0.0).astype(BF16))
    left = jnp.concatenate(parts, axis=0)
    metas = [chunk_ref[n, count * rows :, :].astype(F32) for n in range(group)]
    for i in range(count):
        pieces = []
        for n in range(group):
            back = jnp.exp2(-(metas[n][i : i + 1] + KEPT))
            pieces.append((chunk_ref[n, i * rows : (i + 1) * rows, :].astype(F32) * back).astype(BF16))
        term = dot_nn(left, jnp.concatenate(pieces, axis=0))

        @pl.when(at == 0)
        def _(i=i, term=term):
            sums_ref[i] = term

        @pl.when(at > 0)
        def _(i=i, term=term):
            sums_ref[i] += term

    @pl.when(at == pl.num_programs(0) - 1)
    def _():
        for i in range(count):
            own_ref[i * half : (i + 1) * half, :] = sums_ref[i, :half]
            send_ref[i * half : (i + 1) * half, :] = sums_ref[i, half:].astype(BF16)


def attend(own_ref, got_ref, full_ref, shares_ref, out_ref):
    peers, pair_rows, lanes = out_ref.shape
    channels = lanes // 2
    tokens = full_ref.shape[0]
    tail_ref = full_ref
    half = tokens + channels + 16
    latent = tail_ref[:, :channels]
    scale = tail_ref[:, channels : channels + 1].astype(F32) + tail_ref[:, channels + 1 : channels + 2].astype(F32)
    made = []
    for i in range(3):
        at = i * half
        body = own_ref[at : at + tokens, :] + got_ref[at : at + tokens, :].astype(F32)
        at += tokens
        embed = own_ref[at : at + channels, :] + got_ref[at : at + channels, :].astype(F32)
        at += channels
        shift = own_ref[at : at + 16, :] + got_ref[at : at + 16, :].astype(F32)
        high, low = split_two(embed)
        body = body + dot_nn(latent, high) + dot_nn(latent, low)
        made.append((body * scale + shift[0:1]).astype(BF16))
    queries, keys, values = made
    outs = []
    for h in range(queries.shape[1] // HEAD):
        cols = slice(h * HEAD, (h + 1) * HEAD)
        scores = dot_nt(queries[:, cols], keys[:, cols]) * (1.0 / math.sqrt(HEAD))
        weights = jnp.exp(scores - jnp.max(scores, axis=-1, keepdims=True))
        total = jnp.sum(weights, axis=-1, keepdims=True)
        outs.append((dot_nn(weights.astype(BF16), values[:, cols]) / total).astype(BF16))
    attended = jnp.concatenate(outs, axis=1)
    heads = jnp.sum(shares_ref[...].astype(F32), axis=0)
    high, low = split_two(heads)
    result = dot_nt(attended, high) + dot_nt(attended, low)
    for p in range(peers):
        at = 2 * p * pair_rows
        block = jnp.concatenate([result[at : at + pair_rows], result[at + pair_rows : at + 2 * pair_rows]], axis=1)
        out_ref[p] = block.astype(BF16)


def per_device(
    states, initial, noise_draws, timesteps, context, modulation, out_gate, embed_weight, qkv_weight, out_weight, head_weight
):
    steps, peers = lax.axis_size("tm"), lax.axis_size("seq")
    chips = steps // 2
    mine = lax.axis_index("tm")
    z, core = mine // 2, mine % 2
    tokens_here, channels = initial.shape
    width = context.shape[1]
    rows = qkv_weight.shape[1]
    cols = qkv_weight.shape[2]
    tokens = tokens_here * peers
    half = tokens + channels + 16
    shape = jax.ShapeDtypeStruct

    flip = [(i, i ^ 1) for i in range(steps)]
    same_core = [list(range(0, steps, 2)), list(range(1, steps, 2))]
    reach = chips * rows

    payload, embed_half, mods_mine, mods_other = kernel_call(
        functools.partial(pack_context, rows),
        (
            shape((peers, tokens_here, reach + 128), BF16),
            shape((channels, reach), BF16),
            shape((2, reach), F32),
            shape((2, reach), F32),
        ),
        4,
        1,
        flops=2 * tokens_here * channels * width,
        moved=5000000,
    )(core[None], states[0], embed_weight, context, modulation[0])
    gathered = lax.all_to_all(payload, "seq", 0, 0).reshape(tokens, reach + 128)
    mods_sibling = lax.ppermute(mods_other, "tm", flip)

    chunk, share = kernel_call(
        pack_weights,
        (shape((3 * rows + 16, cols), jnp.int16), shape((channels, cols), BF16)),
        3,
        flops=2 * channels * rows * cols,
        moved=700000,
    )(qkv_weight, out_weight, head_weight)
    head_shares = lax.all_gather(share, "tm")
    chunks = lax.all_gather(chunk, "tm", axis_index_groups=same_core)

    group = min(4, chips)
    span = group * rows
    own, send = pl.pallas_call(
        functools.partial(project, rows),
        grid=(chips // group,),
        out_shape=(shape((3 * half, cols), F32), shape((3 * half, cols), BF16)),
        in_specs=[
            pl.BlockSpec((tokens, span), lambda k: (0, k)),
            pl.BlockSpec((channels, span), lambda k: (0, k)),
            pl.BlockSpec((2, span), lambda k: (0, k)),
            pl.BlockSpec((2, span), lambda k: (0, k)),
            pl.BlockSpec((group, 3 * rows + 16, cols), lambda k: (k, 0, 0)),
        ],
        out_specs=[pl.BlockSpec((3 * half, cols), lambda k: (0, 0))] * 2,
        scratch_shapes=[pltpu.VMEM((3, 2 * half, cols), F32)],
        compiler_params=pltpu.CompilerParams(vmem_limit_bytes=36 * 1024 * 1024),
        cost_estimate=pl.CostEstimate(flops=8000000000, bytes_accessed=10000000, transcendentals=0),
    )(gathered, embed_half, mods_mine, mods_sibling, chunks)
    got = lax.ppermute(send, "tm", flip)

    pair_rows = tokens_here // 2
    whole = lambda *dims: pl.BlockSpec(dims, lambda k: (0,) * len(dims))
    shares = pl.pallas_call(
        attend,
        grid=(1,),
        out_shape=shape((peers, pair_rows, 2 * channels), BF16),
        in_specs=[
            whole(3 * half, cols),
            whole(3 * half, cols),
            pl.BlockSpec((tokens, 128), lambda k: (0, reach // 128)),
            whole(steps, channels, cols),
        ],
        out_specs=whole(peers, pair_rows, 2 * channels),
        compiler_params=pltpu.CompilerParams(vmem_limit_bytes=32 * 1024 * 1024),
        cost_estimate=pl.CostEstimate(flops=600000000, bytes_accessed=4000000, transcendentals=0),
    )(own, got, gathered, head_shares)
    shares = lax.all_to_all(shares, "seq", 0, 0)
    mixed = jnp.sum(shares.astype(F32), axis=0)

    def pairs(value):
        return jnp.concatenate([value[:pair_rows], value[pair_rows:]], axis=1)

    def unpairs(value):
        return jnp.concatenate([value[:, :channels], value[:, channels:]], axis=0)

    gate = jnp.concatenate([out_gate, out_gate], axis=1)
    velocity_f = (1.0 + gate) * mixed
    step_size = sigma_of(timesteps[0, 1]) - sigma_of(timesteps[0, 0])
    drift = step_size * velocity_f + jnp.sqrt(-step_size) * pairs(noise_draws[0])
    both = lax.all_gather(drift, "tm", axis_index_groups=[[2 * i, 2 * i + 1] for i in range(chips)])
    spread = jnp.broadcast_to((both[0] + both[1])[None], (chips, pair_rows, 2 * channels))
    everyone = lax.all_to_all(spread, "tm", 0, 0, axis_index_groups=same_core)
    earlier = lax.broadcasted_iota(jnp.int32, (chips, 1, 1), 0) < z
    before = jnp.sum(jnp.where(earlier, everyone, 0.0), axis=0) + jnp.where(core == 1, both[0], 0.0)
    new_states = initial + unpairs(before)
    return (new_states[None], unpairs(velocity_f).astype(BF16)[None])


def solution(mesh):
    in_specs = (
        P("tm", "seq", None),
        P("seq", None),
        P("tm", "seq", None),
        P("tm", None),
        P("seq", None),
        P("tm", None, None),
        P("tm", None),
        P(),
        P(None, "tm", "seq"),
        P("seq", "tm"),
        P(None, "tm"),
    )
    out_specs = (P("tm", "seq", None), P("tm", "seq", None))
    return jax.shard_map(per_device, mesh=mesh, in_specs=in_specs, out_specs=out_specs, check_vma=False)
```

```python
import functools
import math

import jax
import jax.numpy as jnp
from jax import lax
from jax.experimental import pallas as pl
from jax.experimental.pallas import tpu as pltpu
from jax.sharding import PartitionSpec as P

HEAD = 128
NT = 1000
F32 = jnp.float32
BF16 = jnp.bfloat16
KEPT = 14.0


def sigma_of(level_ids):
    fraction = (level_ids.astype(F32) + 1.0) / NT
    return 5.0 * fraction / (1.0 + 4.0 * fraction)


def dot_nt(a, b):
    return lax.dot_general(a, b, (((1,), (1,)), ((), ())), preferred_element_type=F32)


def dot_nn(a, b):
    return lax.dot_general(a, b, (((1,), (0,)), ((), ())), preferred_element_type=F32)


def split_two(value):
    high = value.astype(BF16)
    return high, (value - high.astype(F32)).astype(BF16)


def kernel_call(body, out_shape, n_in, n_smem=0, flops=0, moved=0, limit=56):
    one = pl.BlockSpec(memory_space=pltpu.VMEM)
    scalar = pl.BlockSpec(memory_space=pltpu.SMEM)
    many = isinstance(out_shape, (tuple, list))
    return pl.pallas_call(
        body,
        out_shape=out_shape,
        in_specs=[scalar] * n_smem + [one] * n_in,
        out_specs=[one] * len(out_shape) if many else one,
        compiler_params=pltpu.CompilerParams(vmem_limit_bytes=limit * 1024 * 1024),
        cost_estimate=pl.CostEstimate(flops=flops, bytes_accessed=moved, transcendentals=0),
    )


def grid_call(body, steps, out_shape, in_specs, out_specs, scratch, flops):
    return pl.pallas_call(
        body,
        grid=(steps,),
        out_shape=out_shape,
        in_specs=in_specs,
        out_specs=out_specs,
        scratch_shapes=scratch,
        compiler_params=pltpu.CompilerParams(vmem_limit_bytes=56 * 1024 * 1024),
        cost_estimate=pl.CostEstimate(flops=flops, bytes_accessed=5000000, transcendentals=0),
    )


def to_whole(weight):
    peak = jnp.maximum(jnp.max(jnp.abs(weight), axis=0, keepdims=True), 1e-30)
    power = jnp.floor(-jnp.log2(peak))
    whole = jnp.round(weight * jnp.exp2(power + KEPT))
    return whole.astype(jnp.int32).astype(jnp.int16), power


def from_whole(whole, power):
    return whole.astype(F32) * jnp.exp2(-(power + KEPT))


def pack_weights(qkv_ref, out_ref, head_ref, chunk_ref):
    count, rows, cols = qkv_ref.shape
    channels = head_ref.shape[0]
    row = lax.broadcasted_iota(jnp.int32, (16, cols), 0)
    meta = jnp.zeros((16, cols), F32)
    for i in range(count):
        chunk_ref[i * rows : (i + 1) * rows, :], power = to_whole(qkv_ref[i].astype(F32))
        meta = jnp.where(row == i, power, meta)
    at = count * rows
    chunk_ref[at : at + channels, :], power = to_whole(dot_nn(head_ref[...], out_ref[...]))
    meta = jnp.where(row == count, power, meta)
    chunk_ref[at + channels :, :] = meta.astype(jnp.int32).astype(jnp.int16)


def pack(rows, core_ref, states_ref, embed_ref, context_ref, mods_ref, *refs):
    weight_refs, (payload_ref, embed_out, mine_ref, other_ref, chunk_ref) = refs[:3], refs[3:]
    peers, tokens, _ = payload_ref.shape
    channels, width = embed_ref.shape
    half = embed_out.shape[1]
    chips = half // rows
    second = core_ref[0] == 1
    latent = states_ref[...].astype(BF16)
    context = context_ref[...].astype(F32)

    def halves(value):
        moved = pltpu.roll(value, width - rows, 1)
        return jnp.where(second, moved, value), jnp.where(second, value, moved)

    def blocks(value, put):
        for j in range(chips):
            put(slice(j * rows, (j + 1) * rows), value[:, 2 * j * rows : (2 * j + 1) * rows])

    def put_context(at, value):
        payload_ref[0, :, at] = value.astype(BF16)

    def put_embed(at, value):
        embed_out[:, at] = value.astype(BF16)

    def put_mine(at, value):
        mine_ref[:, at] = value

    def put_other(at, value):
        other_ref[:, at] = value

    blocks(halves(context)[0], put_context)
    hidden = dot_nn(latent, embed_ref[...]) + context
    scale = lax.rsqrt(jnp.mean(hidden * hidden, axis=-1, keepdims=True) + 1e-06)
    high, low = split_two(scale)
    lane = lax.broadcasted_iota(jnp.int32, (tokens, 128), 1)
    tail = jnp.concatenate([latent.astype(F32), jnp.zeros((tokens, 128 - channels), F32)], axis=1)
    tail = jnp.where(lane == channels, high.astype(F32), tail)
    tail = jnp.where(lane == channels + 1, low.astype(F32), tail)
    payload_ref[0, :, half:] = tail.astype(BF16)
    for p in range(1, peers):
        payload_ref[p] = payload_ref[0]
    blocks(halves(embed_ref[...].astype(F32))[0], put_embed)
    mine, other = halves(mods_ref[...])
    blocks(mine, put_mine)
    blocks(other, put_other)
    pack_weights(*weight_refs, chunk_ref)


def scale_rows(left_ref, context_ref, embed_ref, mods_ref):
    tokens, channels = context_ref.shape[0], embed_ref.shape[0]
    gain = 1.0 + mods_ref[1:2, :]
    left_ref[:tokens, :] = (context_ref[...].astype(F32) * gain).astype(BF16)
    left_ref[tokens : tokens + channels, :] = (embed_ref[...].astype(F32) * gain).astype(BF16)
    row = lax.broadcasted_iota(jnp.int32, (16, gain.shape[1]), 0)
    left_ref[tokens + channels :, :] = jnp.where(row == 0, mods_ref[0:1, :], 0.0).astype(BF16)


def project_sibling(context_ref, embed_ref, mods_ref, chunk_ref, extra_ref, send_ref, weight_ref, heads_ref, left_ref):
    i = pl.program_id(0)
    chips, rows, _ = chunk_ref.shape
    channels = heads_ref.shape[0]
    half = left_ref.shape[0]

    @pl.when(i == 0)
    def _():
        scale_rows(left_ref, context_ref, embed_ref, mods_ref)
        heads = None
        for n in range(chips):
            power = extra_ref[n, channels:, :].astype(F32)[3:4]
            share = from_whole(extra_ref[n, :channels, :], power)
            heads = share if heads is None else heads + share
        heads_ref[...] = heads
        send_ref[3 * half :, :] = heads.astype(BF16)

    row = lax.broadcasted_iota(jnp.int32, (16, heads_ref.shape[1]), 0)
    for n in range(chips):
        meta = extra_ref[n, channels:, :].astype(F32)
        power = jnp.sum(jnp.where(row == i, meta, 0.0), axis=0, keepdims=True)
        weight_ref[0, n * rows : (n + 1) * rows, :] = from_whole(chunk_ref[n], power).astype(BF16)
    result = dot_nn(left_ref[...], weight_ref[0])
    send_ref[pl.ds(pl.multiple_of(i * half, 16), half), :] = result.astype(BF16)


def project_own(context_ref, embed_ref, mods_ref, weight_ref, own_ref, left_ref):
    @pl.when(pl.program_id(0) == 0)
    def _():
        scale_rows(left_ref, context_ref, embed_ref, mods_ref)

    own_ref[...] = dot_nn(left_ref[...], weight_ref[0])


def attend(own_ref, got_ref, full_ref, heads_ref, out_ref):
    peers, pair_rows, lanes = out_ref.shape
    channels = lanes // 2
    tokens = full_ref.shape[0]
    tail_ref = full_ref
    half = tokens + channels + 16
    latent = tail_ref[:, :channels]
    scale = tail_ref[:, channels : channels + 1].astype(F32) + tail_ref[:, channels + 1 : channels + 2].astype(F32)
    made = []
    for i in range(3):
        at = i * half
        body = own_ref[at : at + tokens, :] + got_ref[at : at + tokens, :].astype(F32)
        at += tokens
        embed = own_ref[at : at + channels, :] + got_ref[at : at + channels, :].astype(F32)
        at += channels
        shift = own_ref[at : at + 16, :] + got_ref[at : at + 16, :].astype(F32)
        high, low = split_two(embed)
        body = body + dot_nn(latent, high) + dot_nn(latent, low)
        made.append((body * scale + shift[0:1]).astype(BF16))
    queries, keys, values = made
    outs = []
    for h in range(queries.shape[1] // HEAD):
        cols = slice(h * HEAD, (h + 1) * HEAD)
        scores = dot_nt(queries[:, cols], keys[:, cols]) * (1.0 / math.sqrt(HEAD))
        weights = jnp.exp(scores - jnp.max(scores, axis=-1, keepdims=True))
        total = jnp.sum(weights, axis=-1, keepdims=True)
        outs.append((dot_nn(weights.astype(BF16), values[:, cols]) / total).astype(BF16))
    attended = jnp.concatenate(outs, axis=1)
    heads = heads_ref[...] + got_ref[3 * half :, :].astype(F32)
    high, low = split_two(heads)
    result = dot_nt(attended, high) + dot_nt(attended, low)
    for p in range(peers):
        at = 2 * p * pair_rows
        block = jnp.concatenate([result[at : at + pair_rows], result[at + pair_rows : at + 2 * pair_rows]], axis=1)
        out_ref[p] = block.astype(BF16)


def per_device(
    states, initial, noise_draws, timesteps, context, modulation, out_gate, embed_weight, qkv_weight, out_weight, head_weight
):
    steps, peers = lax.axis_size("tm"), lax.axis_size("seq")
    chips = steps // 2
    mine = lax.axis_index("tm")
    z, core = mine // 2, mine % 2
    tokens_here, channels = initial.shape
    width = context.shape[1]
    rows = qkv_weight.shape[1]
    cols = qkv_weight.shape[2]
    tokens = tokens_here * peers
    half = tokens + channels + 16
    shape = jax.ShapeDtypeStruct

    flip = [(i, i ^ 1) for i in range(steps)]
    same_core = [list(range(0, steps, 2)), list(range(1, steps, 2))]
    reach = chips * rows

    payload, embed_half, mods_mine, mods_other, chunk = kernel_call(
        functools.partial(pack, rows),
        (
            shape((peers, tokens_here, reach + 128), BF16),
            shape((channels, reach), BF16),
            shape((2, reach), F32),
            shape((2, reach), F32),
            shape((3 * rows + channels + 16, cols), jnp.int16),
        ),
        7,
        1,
        flops=2 * tokens_here * channels * width,
        moved=5000000,
    )(core[None], states[0], embed_weight, context, modulation[0], qkv_weight, out_weight.T, head_weight)
    gathered = lax.all_to_all(payload, "seq", 0, 0).reshape(tokens, reach + 128)
    mods_sibling = lax.ppermute(mods_other, "tm", flip)
    chunks = lax.all_gather(chunk, "tm", axis_index_groups=same_core)

    def whole(*dims):
        return pl.BlockSpec(dims, lambda i: (0,) * len(dims))

    extra = channels + 16
    common = [whole(tokens, reach), whole(channels, reach), whole(2, reach)]
    left = [pltpu.VMEM((half, reach), BF16)]
    send, weights, heads = grid_call(
        project_sibling,
        3,
        (shape((3 * half + channels, cols), BF16), shape((3, reach, cols), BF16), shape((channels, cols), F32)),
        common
        + [
            pl.BlockSpec((chips, rows, cols), lambda i: (0, i, 0)),
            pl.BlockSpec((chips, extra, cols), lambda i: (0, 3 * rows // extra, 0)),
        ],
        [whole(3 * half + channels, cols), pl.BlockSpec((1, reach, cols), lambda i: (i, 0, 0)), whole(channels, cols)],
        left,
        4000000000,
    )(gathered, embed_half, mods_sibling, chunks, chunks)
    got = lax.ppermute(send, "tm", flip)
    own = grid_call(
        project_own,
        3,
        shape((3 * half, cols), F32),
        common + [pl.BlockSpec((1, reach, cols), lambda i: (i, 0, 0))],
        pl.BlockSpec((half, cols), lambda i: (i, 0)),
        left,
        4000000000,
    )(gathered, embed_half, mods_mine, weights)

    pair_rows = tokens_here // 2
    shares = grid_call(
        attend,
        1,
        shape((peers, pair_rows, 2 * channels), BF16),
        [
            whole(3 * half, cols),
            whole(3 * half + channels, cols),
            pl.BlockSpec((tokens, 128), lambda i: (0, reach // 128)),
            whole(channels, cols),
        ],
        whole(peers, pair_rows, 2 * channels),
        [],
        600000000,
    )(own, got, gathered, heads)
    shares = lax.all_to_all(shares, "seq", 0, 0)
    mixed = jnp.sum(shares.astype(F32), axis=0)

    def pairs(value):
        return jnp.concatenate([value[:pair_rows], value[pair_rows:]], axis=1)

    def unpairs(value):
        return jnp.concatenate([value[:, :channels], value[:, channels:]], axis=0)

    gate = jnp.concatenate([out_gate, out_gate], axis=1)
    velocity_f = (1.0 + gate) * mixed
    step_size = sigma_of(timesteps[0, 1]) - sigma_of(timesteps[0, 0])
    drift = step_size * velocity_f + jnp.sqrt(-step_size) * pairs(noise_draws[0])
    both = lax.all_gather(drift, "tm", axis_index_groups=[[2 * i, 2 * i + 1] for i in range(chips)])
    spread = jnp.broadcast_to((both[0] + both[1])[None], (chips, pair_rows, 2 * channels))
    everyone = lax.all_to_all(spread, "tm", 0, 0, axis_index_groups=same_core)
    earlier = lax.broadcasted_iota(jnp.int32, (chips, 1, 1), 0) < z
    before = jnp.sum(jnp.where(earlier, everyone, 0.0), axis=0) + jnp.where(core == 1, both[0], 0.0)
    new_states = initial + unpairs(before)
    return (new_states[None], unpairs(velocity_f).astype(BF16)[None])


def solution(mesh):
    in_specs = (
        P("tm", "seq", None),
        P("seq", None),
        P("tm", "seq", None),
        P("tm", None),
        P("seq", None),
        P("tm", None, None),
        P("tm", None),
        P(),
        P(None, "tm", "seq"),
        P("seq", "tm"),
        P(None, "tm"),
    )
    out_specs = (P("tm", "seq", None), P("tm", "seq", None))
    return jax.shard_map(per_device, mesh=mesh, in_specs=in_specs, out_specs=out_specs, check_vma=False)
```

```python
import functools
import math

import jax
import jax.numpy as jnp
from jax import lax
from jax.experimental import pallas as pl
from jax.experimental.pallas import tpu as pltpu
from jax.sharding import PartitionSpec as P

HEAD = 128
NT = 1000
F32 = jnp.float32
BF16 = jnp.bfloat16
KEPT = 14.0
LIMIT = 56 * 1024 * 1024


def sigma_of(level_ids):
    fraction = (level_ids.astype(F32) + 1.0) / NT
    return 5.0 * fraction / (1.0 + 4.0 * fraction)


def dot_nt(a, b):
    return lax.dot_general(a, b, (((1,), (1,)), ((), ())), preferred_element_type=F32)


def dot_nn(a, b):
    return lax.dot_general(a, b, (((1,), (0,)), ((), ())), preferred_element_type=F32)


def split_two(value):
    high = value.astype(BF16)
    return high, (value - high.astype(F32)).astype(BF16)


def to_whole(weight):
    peak = jnp.maximum(jnp.max(jnp.abs(weight), axis=0, keepdims=True), 1e-30)
    power = jnp.floor(-jnp.log2(peak))
    return jnp.round(weight * jnp.exp2(power + KEPT)), power


def from_whole(whole, power):
    return whole.astype(F32) * jnp.exp2(-(power + KEPT))


def whole_block(*dims):
    return pl.BlockSpec(dims, lambda i: (0,) * len(dims))


def grid_call(body, steps, out_shape, in_specs, out_specs, scratch, flops):
    return pl.pallas_call(
        body,
        grid=(steps,),
        out_shape=out_shape,
        in_specs=in_specs,
        out_specs=out_specs,
        scratch_shapes=scratch,
        compiler_params=pltpu.CompilerParams(vmem_limit_bytes=LIMIT),
        cost_estimate=pl.CostEstimate(flops=flops, bytes_accessed=5000000, transcendentals=0),
    )


def pack_weights(odd, qkv_ref, out_ref, head_ref, mine_ref, theirs_ref):
    count, rows, _ = qkv_ref.shape
    channels = head_ref.shape[0]

    def put(at, size, value):
        first, second = value[:, :HEAD], value[:, HEAD:]
        mine_ref[at : at + size, :] = jnp.where(odd, second, first).astype(jnp.int32).astype(jnp.int16)
        theirs_ref[at : at + size, :] = jnp.where(odd, first, second).astype(jnp.int32).astype(jnp.int16)

    row = lax.broadcasted_iota(jnp.int32, (16, 2 * HEAD), 0)
    meta = jnp.zeros((16, 2 * HEAD), F32)
    for i in range(count):
        value, power = to_whole(qkv_ref[i].astype(F32))
        put(i * rows, rows, value)
        meta = jnp.where(row == i, power, meta)
    value, power = to_whole(dot_nn(head_ref[...], out_ref[...]))
    put(count * rows, channels, value)
    put(count * rows + channels, 16, jnp.where(row == count, power, meta))


def pack(rows, place_ref, times_ref, states_ref, gate_ref, embed_ref, context_ref, mods_ref, *refs):
    weight_refs, (payload_ref, embed_out, mods_out, mine_ref, theirs_ref) = refs[:3], refs[3:]
    peers, tokens, _ = payload_ref.shape
    channels, width = embed_ref.shape
    reach = embed_out.shape[1]
    chips = reach // rows
    second, odd = place_ref[0] == 1, place_ref[1] == 1
    latent = states_ref[...].astype(BF16)
    context = context_ref[...].astype(F32)

    def moved(value):
        return pltpu.roll(value, width - rows, 1)

    def blocks(value, put):
        for j in range(chips):
            put(slice(j * rows, (j + 1) * rows), value[:, 2 * j * rows : (2 * j + 1) * rows])

    def mine_of(value):
        return jnp.where(second, moved(value), value)

    def put_context(at, value):
        payload_ref[0, :, at] = value.astype(BF16)

    def put_embed(at, value):
        embed_out[:, at] = value.astype(BF16)

    blocks(mine_of(context), put_context)
    hidden = dot_nn(latent, embed_ref[...]) + context
    scale = lax.rsqrt(jnp.mean(hidden * hidden, axis=-1, keepdims=True) + 1e-06)
    high, low = split_two(scale)
    lane = lax.broadcasted_iota(jnp.int32, (tokens, 128), 1)
    tail = jnp.concatenate([latent.astype(F32), jnp.zeros((tokens, 128 - channels), F32)], axis=1)
    tail = jnp.where(lane == channels, high.astype(F32), tail)
    tail = jnp.where(lane == channels + 1, low.astype(F32), tail)
    payload_ref[0, :, reach:] = tail.astype(BF16)
    for p in range(1, peers):
        payload_ref[p] = payload_ref[0]
    blocks(mine_of(embed_ref[...].astype(F32)), put_embed)
    now = jnp.full((1, channels), times_ref[0, 0], jnp.int32)
    later = jnp.full((1, channels), times_ref[0, 1], jnp.int32)
    factor = (sigma_of(later) - sigma_of(now)) * (1.0 + gate_ref[...])
    for core in range(2):
        value = moved(mods_ref[...]) if core else mods_ref[...]

        def put_mods(at, part, core=core):
            mods_out[core, 0:2, at] = part
            mods_out[core + 2, 0:2, at] = part

        blocks(value, put_mods)
        for p in (core, core + 2):
            mods_out[p, 2:4, :] = jnp.zeros((2, reach), F32)
            mods_out[p, 2:3, :channels] = factor
    pack_weights(odd, *weight_refs, mine_ref, theirs_ref)


def scale_rows(left_ref, context_ref, embed_ref, mods):
    tokens, channels = context_ref.shape[0], embed_ref.shape[0]
    gain = 1.0 + mods[1:2, :]
    left_ref[:tokens, :] = (context_ref[...].astype(F32) * gain).astype(BF16)
    left_ref[tokens : tokens + channels, :] = (embed_ref[...].astype(F32) * gain).astype(BF16)
    row = lax.broadcasted_iota(jnp.int32, (16, gain.shape[1]), 0)
    left_ref[tokens + channels :, :] = jnp.where(row == 0, mods[0:1, :], 0.0).astype(BF16)


def project_sent(rows, place_ref, context_ref, embed_ref, mods_ref, chunk_ref, send_ref, weight_ref, heads_ref, left_ref):
    at = pl.program_id(0)
    odd = place_ref[1]
    channels = heads_ref.shape[0]
    half = left_ref.shape[0]
    scale_rows(left_ref, context_ref, embed_ref, mods_ref[place_ref[2 + at]])

    @pl.when(at == 0)
    def _():
        heads = None
        for q in range(2 * chunk_ref.shape[0]):
            block = chunk_ref[q // 2, (q % 2 + odd) % 2]
            meta = block[3 * rows + channels :, :].astype(F32)
            for i in range(3):
                part = from_whole(block[i * rows : (i + 1) * rows, :], meta[i : i + 1])
                weight_ref[q * rows : (q + 1) * rows, i * HEAD : (i + 1) * HEAD] = part.astype(BF16)
            share = from_whole(block[3 * rows : 3 * rows + channels, :], meta[3:4])
            heads = share if heads is None else heads + share
        heads_ref[...] = heads
        send_ref[2 * half :, :HEAD] = heads.astype(BF16)
        send_ref[2 * half :, HEAD:] = jnp.zeros((channels, 2 * HEAD), BF16)

    result = dot_nn(left_ref[...], weight_ref[...])
    send_ref[pl.ds(pl.multiple_of(at * half, 16), half), :] = result.astype(BF16)


def project_kept(place_ref, context_ref, embed_ref, mods_ref, weight_ref, own_ref, left_ref):
    scale_rows(left_ref, context_ref, embed_ref, mods_ref[place_ref[4 + pl.program_id(0)]])
    own_ref[...] = dot_nn(left_ref[...], weight_ref[...])


def attend(own_ref, got_ref, tail_ref, other_ref, heads_ref, out_ref):
    peers, tokens_here, lanes = out_ref.shape
    channels = lanes // 2
    tokens = tail_ref.shape[0]
    half = tokens + channels + 16
    heads = heads_ref[...] + got_ref[2 * half :, :HEAD].astype(F32)
    heads_high, heads_low = split_two(heads)
    results = []
    for step, ref in enumerate((tail_ref, other_ref)):
        latent = ref[:, :channels]
        scale = ref[:, channels : channels + 1].astype(F32) + ref[:, channels + 1 : channels + 2].astype(F32)
        at = step * half
        body = own_ref[at : at + tokens, :] + got_ref[at : at + tokens, :].astype(F32)
        at += tokens
        high, low = split_two(own_ref[at : at + channels, :] + got_ref[at : at + channels, :].astype(F32))
        at += channels
        shift = own_ref[at : at + 16, :] + got_ref[at : at + 16, :].astype(F32)
        body = body + dot_nn(latent, high) + dot_nn(latent, low)
        made = (body * scale + shift[0:1]).astype(BF16)
        queries, keys, values = (made[:, i * HEAD : (i + 1) * HEAD] for i in range(3))
        scores = dot_nt(queries, keys) * (1.0 / math.sqrt(HEAD))
        weights = jnp.exp(scores - jnp.max(scores, axis=-1, keepdims=True))
        total = jnp.sum(weights, axis=-1, keepdims=True)
        attended = (dot_nn(weights.astype(BF16), values) / total).astype(BF16)
        results.append(dot_nt(attended, heads_high) + dot_nt(attended, heads_low))
    result = jnp.concatenate(results, axis=1).astype(BF16)
    for p in range(peers):
        out_ref[p] = result[p * tokens_here : (p + 1) * tokens_here]


def per_device(
    states, initial, noise_draws, timesteps, context, modulation, out_gate, embed_weight, qkv_weight, out_weight, head_weight
):
    steps, peers = lax.axis_size("tm"), lax.axis_size("seq")
    chips = steps // 2
    mine = lax.axis_index("tm")
    z, core = mine // 2, mine % 2
    odd = z % 2
    tokens_here, channels = initial.shape
    rows = qkv_weight.shape[1]
    tokens = tokens_here * peers
    half = tokens + channels + 16
    reach = chips * rows
    shape = jax.ShapeDtypeStruct

    flip = [(i, i ^ 1) for i in range(steps)]
    across = [(i, i ^ 2) for i in range(steps)]
    fours = [list(range(4 * i, 4 * i + 4)) for i in range(steps // 4)]
    same_head = [[4 * n + 2 * h + c for n in range(chips // 2)] for h in range(2) for c in range(2)]
    same_core = [list(range(0, steps, 2)), list(range(1, steps, 2))]
    spot = mine % 4
    place = jnp.stack([core, odd, spot ^ 1, spot ^ 3, spot, spot ^ 2]).astype(jnp.int32)

    one = pl.BlockSpec(memory_space=pltpu.VMEM)
    scalar = pl.BlockSpec(memory_space=pltpu.SMEM)
    block_rows = 3 * rows + channels + 16
    payload, embed_half, mods_out, chunk, theirs = pl.pallas_call(
        functools.partial(pack, rows),
        out_shape=(
            shape((peers, tokens_here, reach + 128), BF16),
            shape((channels, reach), BF16),
            shape((4, 4, reach), F32),
            shape((block_rows, HEAD), jnp.int16),
            shape((block_rows, HEAD), jnp.int16),
        ),
        in_specs=[scalar] * 2 + [one] * 8,
        out_specs=[one] * 5,
        compiler_params=pltpu.CompilerParams(vmem_limit_bytes=LIMIT),
        cost_estimate=pl.CostEstimate(flops=30000000, bytes_accessed=5000000, transcendentals=0),
    )(place, timesteps, states[0], out_gate, embed_weight, context, modulation[0], qkv_weight, out_weight.T, head_weight)
    received = lax.ppermute(theirs, "tm", across)
    gathered = lax.all_to_all(payload, "seq", 0, 0).reshape(tokens, reach + 128)
    mods = lax.all_to_all(mods_out, "tm", 0, 0, axis_index_groups=fours)
    both = jnp.concatenate([chunk, received], axis=0)
    chunks = lax.all_gather(both, "tm", axis_index_groups=same_head).reshape(chips // 2, 2, block_rows, HEAD)

    width = 3 * HEAD
    common = [scalar, whole_block(tokens, reach), whole_block(channels, reach), whole_block(4, 4, reach)]
    left = [pltpu.VMEM((half, reach), BF16)]
    send, weights, heads = grid_call(
        functools.partial(project_sent, rows),
        2,
        (shape((2 * half + channels, width), BF16), shape((reach, width), BF16), shape((channels, HEAD), F32)),
        common + [whole_block(chips // 2, 2, block_rows, HEAD)],
        [whole_block(2 * half + channels, width), whole_block(reach, width), whole_block(channels, HEAD)],
        left,
        4000000000,
    )(place, gathered, embed_half, mods, chunks)
    got = lax.ppermute(send, "tm", flip)
    other_tail = lax.ppermute(gathered[:, reach:], "tm", across)
    own = grid_call(
        project_kept,
        2,
        shape((2 * half, width), F32),
        common + [whole_block(reach, width)],
        pl.BlockSpec((half, width), lambda i: (i, 0)),
        left,
        4000000000,
    )(place, gathered, embed_half, mods, weights)

    shares = grid_call(
        attend,
        1,
        shape((peers, tokens_here, 2 * channels), BF16),
        [
            whole_block(2 * half, width),
            whole_block(2 * half + channels, width),
            pl.BlockSpec((tokens, 128), lambda i: (0, reach // 128)),
            whole_block(tokens, 128),
            whole_block(channels, HEAD),
        ],
        whole_block(peers, tokens_here, 2 * channels),
        [],
        600000000,
    )(own, got, gathered, other_tail, heads)
    shares = lax.all_to_all(shares, "seq", 0, 0)
    mixed = jnp.sum(shares.astype(F32), axis=0)

    step_size = sigma_of(timesteps[0, 1]) - sigma_of(timesteps[0, 0])
    gain = 1.0 + out_gate
    factors = jnp.concatenate([step_size * gain, lax.dynamic_slice(mods, (spot ^ 2, 2, 0), (1, 1, channels))[0]], axis=1)
    kicks = jnp.sqrt(-step_size) * noise_draws[0]
    drifts = factors * mixed + jnp.pad(kicks, ((0, 0), (0, channels)))
    rest = lax.ppermute(mixed[:, channels:], "tm", across)
    pair = lax.all_gather(drifts, "tm", axis_index_groups=[[2 * i, 2 * i + 1] for i in range(chips)])
    spread = jnp.broadcast_to((pair[0] + pair[1]).astype(BF16)[None], (chips, tokens_here, 2 * channels))
    everyone = lax.all_to_all(spread, "tm", 0, 0, axis_index_groups=same_core).astype(F32)
    velocity_f = gain * (mixed[:, :channels] + rest)
    drift = step_size * velocity_f + kicks
    place_z = lax.broadcasted_iota(jnp.int32, (chips, 1, 1), 0)
    second = (core == 1).astype(F32)

    def weight_of(chip):
        return jnp.where(chip < z, 1.0, jnp.where(chip == z, second, 0.0))

    before = jnp.sum(
        everyone[:, :, :channels] * weight_of(place_z) + everyone[:, :, channels:] * weight_of(place_z ^ 1), axis=0
    )
    new_states = initial + (before - second * drift)
    return (new_states[None], velocity_f.astype(BF16)[None])


def solution(mesh):
    in_specs = (
        P("tm", "seq", None),
        P("seq", None),
        P("tm", "seq", None),
        P("tm", None),
        P("seq", None),
        P("tm", None, None),
        P("tm", None),
        P(),
        P(None, "tm", "seq"),
        P("seq", "tm"),
        P(None, "tm"),
    )
    out_specs = (P("tm", "seq", None), P("tm", "seq", None))
    return jax.shard_map(per_device, mesh=mesh, in_specs=in_specs, out_specs=out_specs, check_vma=False)
```

```python
import math

import jax
import jax.numpy as jnp
from jax import lax
from jax.experimental import pallas as pl
from jax.experimental.pallas import tpu as pltpu
from jax.sharding import PartitionSpec as P

HEAD = 128
NT = 1000
F32 = jnp.float32
BF16 = jnp.bfloat16
KEPT = 14.0
LIMIT = 56 * 1024 * 1024


def sigma_of(level_ids):
    fraction = (level_ids.astype(F32) + 1.0) / NT
    return 5.0 * fraction / (1.0 + 4.0 * fraction)


def dot_nt(a, b):
    return lax.dot_general(a, b, (((1,), (1,)), ((), ())), preferred_element_type=F32)


def dot_nn(a, b):
    return lax.dot_general(a, b, (((1,), (0,)), ((), ())), preferred_element_type=F32)


def split_two(value):
    high = value.astype(BF16)
    return high, (value - high.astype(F32)).astype(BF16)


def to_whole(weight):
    peak = jnp.maximum(jnp.max(jnp.abs(weight), axis=0, keepdims=True), 1e-30)
    power = jnp.floor(-jnp.log2(peak))
    whole = jnp.round(weight * jnp.exp2(power + KEPT))
    return whole.astype(jnp.int32).astype(jnp.int16), power


def from_whole(whole, power):
    return whole.astype(F32) * jnp.exp2(-(power + KEPT))


def pack_weights(qkv_ref, out_ref, head_ref, chunk_ref):
    count, rows, cols = qkv_ref.shape
    channels = head_ref.shape[0]
    row = lax.broadcasted_iota(jnp.int32, (16, cols), 0)
    meta = jnp.zeros((16, cols), F32)
    for i in range(count):
        chunk_ref[i * rows : (i + 1) * rows, :], power = to_whole(qkv_ref[i].astype(F32))
        meta = jnp.where(row == i, power, meta)
    at = count * rows
    chunk_ref[at : at + channels, :], power = to_whole(dot_nn(head_ref[...], out_ref[...]))
    meta = jnp.where(row == count, power, meta)
    chunk_ref[at + channels :, :] = meta.astype(jnp.int32).astype(jnp.int16)


def pack(core_ref, times_ref, states_ref, gate_ref, embed_ref, context_ref, *refs):
    weight_refs, (payload_ref, factors_ref, chunk_ref) = refs[:3], refs[3:]
    peers, tokens, lanes = payload_ref.shape
    channels = embed_ref.shape[0]
    half = lanes - 128
    here = pl.ds(pl.multiple_of(core_ref[0] * half, 128), half)
    latent = states_ref[...].astype(BF16)
    payload_ref[0, :, :half] = context_ref[:, here]
    hidden = dot_nn(latent, embed_ref[...]) + context_ref[...].astype(F32)
    scale = lax.rsqrt(jnp.mean(hidden * hidden, axis=-1, keepdims=True) + 1e-06)
    high, low = split_two(scale)
    lane = lax.broadcasted_iota(jnp.int32, (tokens, 128), 1)
    tail = jnp.concatenate([latent.astype(F32), jnp.zeros((tokens, 128 - channels), F32)], axis=1)
    tail = jnp.where(lane == channels, high.astype(F32), tail)
    tail = jnp.where(lane == channels + 1, low.astype(F32), tail)
    payload_ref[0, :, half:] = tail.astype(BF16)
    for p in range(1, peers):
        payload_ref[p] = payload_ref[0]
    gain = 1.0 + jnp.concatenate([gate_ref[...], gate_ref[...]], axis=1)
    now = jnp.full(gain.shape, times_ref[0, 0], jnp.int32)
    later = jnp.full(gain.shape, times_ref[0, 1], jnp.int32)
    step_size = sigma_of(later) - sigma_of(now)
    row = lax.broadcasted_iota(jnp.int32, (8, gain.shape[1]), 0)
    factors_ref[...] = jnp.where(row == 0, gain, jnp.where(row == 1, step_size, jnp.sqrt(-step_size)))
    pack_weights(*weight_refs, chunk_ref)


def after(value, other):
    anywhere = pl.BlockSpec(memory_space=pl.ANY)
    return pl.pallas_call(
        lambda value_ref, other_ref, out_ref: None,
        out_shape=jax.ShapeDtypeStruct(value.shape, value.dtype),
        in_specs=[anywhere, anywhere],
        out_specs=anywhere,
        input_output_aliases={0: 0},
    )(value, other)


def scale_rows(left_ref, context_ref, embed_ref, mods_ref):
    tokens, channels = context_ref.shape[0], embed_ref.shape[0]
    gain = 1.0 + mods_ref[1:2, :]
    left_ref[:tokens, :] = (context_ref[...].astype(F32) * gain).astype(BF16)
    left_ref[tokens : tokens + channels, :] = (embed_ref[...].astype(F32) * gain).astype(BF16)
    row = lax.broadcasted_iota(jnp.int32, (16, gain.shape[1]), 0)
    left_ref[tokens + channels :, :] = jnp.where(row == 0, mods_ref[0:1, :], 0.0).astype(BF16)


def product(i, chunk_ref, extra_ref, left_ref, weight_ref):
    chips, rows, cols = chunk_ref.shape
    row = lax.broadcasted_iota(jnp.int32, (16, cols), 0)
    for n in range(chips):
        meta = extra_ref[n, extra_ref.shape[1] - 16 :, :].astype(F32)
        power = jnp.sum(jnp.where(row == i, meta, 0.0), axis=0, keepdims=True)
        weight_ref[n * rows : (n + 1) * rows, :] = from_whole(chunk_ref[n], power).astype(BF16)
    return dot_nn(left_ref[...], weight_ref[...])


def head_shares(extra_ref):
    channels = extra_ref.shape[1] - 16
    heads = None
    for n in range(extra_ref.shape[0]):
        power = extra_ref[n, channels:, :].astype(F32)[3:4]
        share = from_whole(extra_ref[n, :channels, :], power)
        heads = share if heads is None else heads + share
    return heads


def first_half(
    place_ref, context_ref, embed_ref, mods_ref, chunk_ref, extra_ref, sums_ref, heads_ref, left_ref, weight_ref
):
    i = pl.program_id(0)

    @pl.when(i == 0)
    def _():
        scale_rows(left_ref, context_ref, embed_ref, mods_ref)
        heads_ref[...] = head_shares(extra_ref)

    sums_ref[...] = product(i, chunk_ref, extra_ref, left_ref, weight_ref)


def second_half(
    place_ref,
    context_ref,
    embed_ref,
    mods_ref,
    chunk_ref,
    extra_ref,
    sums_ref,
    heads_ref,
    tail_ref,
    out_ref,
    left_ref,
    weight_ref,
    made_ref,
):
    i = pl.program_id(0)
    tokens, channels = context_ref.shape[0], embed_ref.shape[0]

    @pl.when(i == 0)
    def _():
        scale_rows(left_ref, context_ref, embed_ref, mods_ref)

    total = sums_ref[...] + product(i, chunk_ref, extra_ref, left_ref, weight_ref)
    latent = tail_ref[:, :channels]
    scale = tail_ref[:, channels : channels + 1].astype(F32) + tail_ref[:, channels + 1 : channels + 2].astype(F32)
    high, low = split_two(total[tokens : tokens + channels])
    body = total[:tokens] + dot_nn(latent, high) + dot_nn(latent, low)
    made_ref[i] = (body * scale + total[tokens + channels : tokens + channels + 1]).astype(BF16)

    @pl.when(i == pl.num_programs(0) - 1)
    def _():
        outs = []
        for h in range(made_ref.shape[2] // HEAD):
            cols = slice(h * HEAD, (h + 1) * HEAD)
            scores = dot_nt(made_ref[0, :, cols], made_ref[1, :, cols]) * (1.0 / math.sqrt(HEAD))
            weights = jnp.exp(scores - jnp.max(scores, axis=-1, keepdims=True))
            norm = jnp.sum(weights, axis=-1, keepdims=True)
            outs.append((dot_nn(weights.astype(BF16), made_ref[2, :, cols]) / norm).astype(BF16))
        attended = jnp.concatenate(outs, axis=1)
        head_high, head_low = split_two(heads_ref[...] + head_shares(extra_ref))
        result = dot_nt(attended, head_high) + dot_nt(attended, head_low)
        peers, pair_rows, _ = out_ref.shape
        for p in range(peers):
            at = 2 * p * pair_rows
            block = jnp.concatenate([result[at : at + pair_rows], result[at + pair_rows : at + 2 * pair_rows]], axis=1)
            out_ref[p] = block.astype(BF16)


def per_device(
    states, initial, noise_draws, timesteps, context, modulation, out_gate, embed_weight, qkv_weight, out_weight, head_weight
):
    steps, peers = lax.axis_size("tm"), lax.axis_size("seq")
    chips = steps // 2
    mine = lax.axis_index("tm")
    z, core = mine >> 1, mine & 1
    tokens_here, channels = initial.shape
    rows, cols = qkv_weight.shape[1:]
    tokens = tokens_here * peers
    half = tokens + channels + 16
    reach = chips * rows
    extra = channels + 16
    shape = jax.ShapeDtypeStruct
    place = core[None]

    flip = [(i, i ^ 1) for i in range(steps)]
    same_core = [list(range(0, steps, 2)), list(range(1, steps, 2))]
    one = pl.BlockSpec(memory_space=pltpu.VMEM)
    scalar = pl.BlockSpec(memory_space=pltpu.SMEM)
    params = pltpu.CompilerParams(vmem_limit_bytes=LIMIT)

    payload, factors, chunk = pl.pallas_call(
        pack,
        out_shape=(
            shape((peers, tokens_here, reach + 128), BF16),
            shape((8, 2 * channels), F32),
            shape((3 * rows + extra, cols), jnp.int16),
        ),
        in_specs=[scalar] * 2 + [one] * 7,
        out_specs=[one] * 3,
        compiler_params=params,
        cost_estimate=pl.CostEstimate(flops=30000000, bytes_accessed=5000000, transcendentals=0),
    )(place, timesteps, states[0], out_gate, embed_weight, context, qkv_weight, out_weight.T, head_weight)
    gathered = lax.all_to_all(payload, "seq", 0, 0).reshape(tokens, reach + 128)
    chunks = lax.all_gather(chunk, "tm")
    gathered = after(gathered, chunks)
    flipped = lax.ppermute(gathered, "tm", flip)

    def fixed(*dims):
        return pl.BlockSpec(dims, lambda i, place: (0,) * len(dims))

    def halved(body, at, more_in, out_shape, out_specs, scratch):
        return pl.pallas_call(
            body,
            out_shape=out_shape,
            grid_spec=pltpu.PrefetchScalarGridSpec(
                num_scalar_prefetch=1,
                grid=(3,),
                in_specs=[
                    fixed(tokens, reach),
                    pl.BlockSpec((channels, reach), lambda i, place: (0, at(place[0]))),
                    pl.BlockSpec((2, reach), lambda i, place: (0, at(place[0]))),
                    pl.BlockSpec((chips, rows, cols), lambda i, place: (at(place[0]), i, 0)),
                    pl.BlockSpec((chips, extra, cols), lambda i, place: (at(place[0]), 3 * rows // extra, 0)),
                ]
                + more_in,
                out_specs=out_specs,
                scratch_shapes=[pltpu.VMEM((half, reach), BF16), pltpu.VMEM((reach, cols), BF16)] + scratch,
            ),
            compiler_params=pltpu.CompilerParams(vmem_limit_bytes=32 * 1024 * 1024),
            cost_estimate=pl.CostEstimate(flops=4000000000, bytes_accessed=9000000, transcendentals=0),
        )

    by_kind = pl.BlockSpec((half, cols), lambda i, place: (i, 0))
    sums, heads = halved(
        first_half,
        lambda c: c,
        [],
        (shape((3 * half, cols), F32), shape((channels, cols), F32)),
        [by_kind, fixed(channels, cols)],
        [],
    )(place, gathered, embed_weight, modulation[0], chunks, chunks)
    pair_rows = tokens_here // 2
    shares = halved(
        second_half,
        lambda c: 1 - c,
        [by_kind, fixed(channels, cols), pl.BlockSpec((tokens, 128), lambda i, place: (0, reach // 128))],
        shape((peers, pair_rows, 2 * channels), BF16),
        fixed(peers, pair_rows, 2 * channels),
        [pltpu.VMEM((3, tokens, cols), BF16)],
    )(place, flipped, embed_weight, modulation[0], chunks, chunks, sums, heads, gathered)
    shares = lax.all_to_all(shares, "seq", 0, 0)
    mixed = jnp.sum(shares.astype(F32), axis=0)

    def pairs(value):
        return jnp.concatenate([value[:pair_rows], value[pair_rows:]], axis=1)

    def unpairs(value):
        return jnp.concatenate([value[:, :channels], value[:, channels:]], axis=0)

    velocity_f = factors[0:1] * mixed
    drift = factors[1:2] * velocity_f + factors[2:3] * pairs(noise_draws[0])
    both = lax.all_gather(drift, "tm", axis_index_groups=[[2 * i, 2 * i + 1] for i in range(chips)])
    spread = jnp.broadcast_to((both[0] + both[1]).astype(BF16)[None], (chips, pair_rows, 2 * channels))
    everyone = lax.all_to_all(spread, "tm", 0, 0, axis_index_groups=same_core).astype(F32)
    earlier = lax.broadcasted_iota(jnp.int32, (chips, 1, 1), 0) < z
    before = jnp.sum(jnp.where(earlier, everyone, 0.0), axis=0) + jnp.where(core == 1, both[0], 0.0)
    new_states = initial + unpairs(before)
    return (new_states[None], unpairs(velocity_f).astype(BF16)[None])


def solution(mesh):
    in_specs = (
        P("tm", "seq", None),
        P("seq", None),
        P("tm", "seq", None),
        P("tm", None),
        P("seq", None),
        P("tm", None, None),
        P("tm", None),
        P(),
        P(None, "tm", "seq"),
        P("seq", "tm"),
        P(None, "tm"),
    )
    out_specs = (P("tm", "seq", None), P("tm", "seq", None))
    return jax.shard_map(per_device, mesh=mesh, in_specs=in_specs, out_specs=out_specs, check_vma=False)
```

```python
import math

import jax
import jax.numpy as jnp
from jax import lax
from jax.experimental import pallas as pl
from jax.experimental.pallas import tpu as pltpu
from jax.sharding import PartitionSpec as P

HEAD = 128
NT = 1000
F32 = jnp.float32
BF16 = jnp.bfloat16
KEPT = 14.0
LIMIT = 56 * 1024 * 1024


def sigma_of(level_ids):
    fraction = (level_ids.astype(F32) + 1.0) / NT
    return 5.0 * fraction / (1.0 + 4.0 * fraction)


def dot_nt(a, b):
    return lax.dot_general(a, b, (((1,), (1,)), ((), ())), preferred_element_type=F32)


def dot_nn(a, b):
    return lax.dot_general(a, b, (((1,), (0,)), ((), ())), preferred_element_type=F32)


def split_two(value):
    high = value.astype(BF16)
    return high, (value - high.astype(F32)).astype(BF16)


def to_whole(weight):
    peak = jnp.maximum(jnp.max(jnp.abs(weight), axis=0, keepdims=True), 1e-30)
    power = jnp.floor(-jnp.log2(peak))
    whole = jnp.round(weight * jnp.exp2(power + KEPT))
    return whole.astype(jnp.int32).astype(jnp.int16), power


def from_whole(whole, power):
    return whole.astype(F32) * jnp.exp2(-(power + KEPT))


def pack_weights(qkv_ref, out_ref, head_ref, chunk_ref):
    count, rows, cols = qkv_ref.shape
    channels = head_ref.shape[0]
    row = lax.broadcasted_iota(jnp.int32, (16, cols), 0)
    meta = jnp.zeros((16, cols), F32)
    for i in range(count):
        chunk_ref[i * rows : (i + 1) * rows, :], power = to_whole(qkv_ref[i].astype(F32))
        meta = jnp.where(row == i, power, meta)
    at = count * rows
    chunk_ref[at : at + channels, :], power = to_whole(dot_nn(head_ref[...], out_ref[...]))
    meta = jnp.where(row == count, power, meta)
    chunk_ref[at + channels :, :] = meta.astype(jnp.int32).astype(jnp.int16)


def pack(core_ref, times_ref, states_ref, noise_ref, gate_ref, embed_ref, context_ref, *refs):
    weight_refs, (payload_ref, gains_ref, sizes_ref, kicks_ref, chunk_ref) = refs[:3], refs[3:]
    peers, tokens, lanes = payload_ref.shape
    channels = embed_ref.shape[0]
    half = lanes - 128
    here = pl.ds(pl.multiple_of(core_ref[0] * half, 128), half)
    latent = states_ref[...].astype(BF16)
    payload_ref[0, :, :half] = context_ref[:, here]
    hidden = dot_nn(latent, embed_ref[...]) + context_ref[...].astype(F32)
    scale = lax.rsqrt(jnp.mean(hidden * hidden, axis=-1, keepdims=True) + 1e-06)
    high, low = split_two(scale)
    lane = lax.broadcasted_iota(jnp.int32, (tokens, 128), 1)
    tail = jnp.concatenate([latent.astype(F32), jnp.zeros((tokens, 128 - channels), F32)], axis=1)
    tail = jnp.where(lane == channels, high.astype(F32), tail)
    tail = jnp.where(lane == channels + 1, low.astype(F32), tail)
    payload_ref[0, :, half:] = tail.astype(BF16)
    for p in range(1, peers):
        payload_ref[p] = payload_ref[0]
    gain = 1.0 + jnp.concatenate([gate_ref[...], gate_ref[...]], axis=1)
    now = jnp.full(gain.shape, times_ref[0, 0], jnp.int32)
    later = jnp.full(gain.shape, times_ref[0, 1], jnp.int32)
    step_size = sigma_of(later) - sigma_of(now)
    gains_ref[...] = jnp.broadcast_to(gain, gains_ref.shape)
    sizes_ref[...] = jnp.broadcast_to(step_size, sizes_ref.shape)
    pair_rows = tokens // 2
    noise = jnp.concatenate([noise_ref[:pair_rows], noise_ref[pair_rows:]], axis=1)
    kicks_ref[...] = jnp.sqrt(-step_size) * noise
    pack_weights(*weight_refs, chunk_ref)


def scale_rows(left_ref, context_ref, embed_ref, mods_ref):
    tokens, channels = context_ref.shape[0], embed_ref.shape[0]
    gain = 1.0 + mods_ref[1:2, :]
    left_ref[:tokens, :] = (context_ref[...].astype(F32) * gain).astype(BF16)
    left_ref[tokens : tokens + channels, :] = (embed_ref[...].astype(F32) * gain).astype(BF16)
    row = lax.broadcasted_iota(jnp.int32, (16, gain.shape[1]), 0)
    left_ref[tokens + channels :, :] = jnp.where(row == 0, mods_ref[0:1, :], 0.0).astype(BF16)


def product(i, chunk_ref, extra_ref, left_ref, weight_ref):
    chips, rows, cols = chunk_ref.shape
    row = lax.broadcasted_iota(jnp.int32, (16, cols), 0)
    for n in range(chips):
        meta = extra_ref[n, extra_ref.shape[1] - 16 :, :].astype(F32)
        power = jnp.sum(jnp.where(row == i, meta, 0.0), axis=0, keepdims=True)
        weight_ref[n * rows : (n + 1) * rows, :] = from_whole(chunk_ref[n], power).astype(BF16)
    return dot_nn(left_ref[...], weight_ref[...])


def head_shares(extra_ref):
    channels = extra_ref.shape[1] - 16
    heads = None
    for n in range(extra_ref.shape[0]):
        power = extra_ref[n, channels:, :].astype(F32)[3:4]
        share = from_whole(extra_ref[n, :channels, :], power)
        heads = share if heads is None else heads + share
    return heads


def first_half(
    place_ref, context_ref, embed_ref, mods_ref, chunk_ref, extra_ref, sums_ref, heads_ref, left_ref, weight_ref
):
    i = pl.program_id(0)

    @pl.when(i == 0)
    def _():
        scale_rows(left_ref, context_ref, embed_ref, mods_ref)
        heads_ref[...] = head_shares(extra_ref)

    sums_ref[...] = product(i, chunk_ref, extra_ref, left_ref, weight_ref)


def second_half(
    place_ref,
    context_ref,
    embed_ref,
    mods_ref,
    chunk_ref,
    extra_ref,
    sums_ref,
    heads_ref,
    tail_ref,
    out_ref,
    left_ref,
    weight_ref,
    made_ref,
):
    i = pl.program_id(0)
    tokens, channels = context_ref.shape[0], embed_ref.shape[0]

    @pl.when(i == 0)
    def _():
        scale_rows(left_ref, context_ref, embed_ref, mods_ref)

    total = sums_ref[...] + product(i, chunk_ref, extra_ref, left_ref, weight_ref)
    latent = tail_ref[:, :channels]
    scale = tail_ref[:, channels : channels + 1].astype(F32) + tail_ref[:, channels + 1 : channels + 2].astype(F32)
    high, low = split_two(total[tokens : tokens + channels])
    body = total[:tokens] + dot_nn(latent, high) + dot_nn(latent, low)
    made_ref[i] = (body * scale + total[tokens + channels : tokens + channels + 1]).astype(BF16)

    @pl.when(i == pl.num_programs(0) - 1)
    def _():
        outs = []
        for h in range(made_ref.shape[2] // HEAD):
            cols = slice(h * HEAD, (h + 1) * HEAD)
            scores = dot_nt(made_ref[0, :, cols], made_ref[1, :, cols]) * (1.0 / math.sqrt(HEAD))
            weights = jnp.exp(scores - jnp.max(scores, axis=-1, keepdims=True))
            norm = jnp.sum(weights, axis=-1, keepdims=True)
            outs.append((dot_nn(weights.astype(BF16), made_ref[2, :, cols]) / norm).astype(BF16))
        attended = jnp.concatenate(outs, axis=1)
        head_high, head_low = split_two(heads_ref[...] + head_shares(extra_ref))
        result = dot_nt(attended, head_high) + dot_nt(attended, head_low)
        peers, pair_rows, _ = out_ref.shape
        for p in range(peers):
            at = 2 * p * pair_rows
            block = jnp.concatenate([result[at : at + pair_rows], result[at + pair_rows : at + 2 * pair_rows]], axis=1)
            out_ref[p] = block.astype(BF16)


def per_device(
    states, initial, noise_draws, timesteps, context, modulation, out_gate, embed_weight, qkv_weight, out_weight, head_weight
):
    steps, peers = lax.axis_size("tm"), lax.axis_size("seq")
    chips = steps // 2
    mine = lax.axis_index("tm")
    z, core = mine >> 1, mine & 1
    tokens_here, channels = initial.shape
    rows, cols = qkv_weight.shape[1:]
    tokens = tokens_here * peers
    half = tokens + channels + 16
    reach = chips * rows
    extra = channels + 16
    shape = jax.ShapeDtypeStruct
    place = core[None]

    flip = [(i, i ^ 1) for i in range(steps)]
    same_core = [list(range(0, steps, 2)), list(range(1, steps, 2))]
    one = pl.BlockSpec(memory_space=pltpu.VMEM)
    scalar = pl.BlockSpec(memory_space=pltpu.SMEM)
    params = pltpu.CompilerParams(vmem_limit_bytes=LIMIT)

    pair_rows = tokens_here // 2
    payload, gains, sizes, kicks, chunk = pl.pallas_call(
        pack,
        out_shape=(
            shape((peers, tokens_here, reach + 128), BF16),
            shape((pair_rows, 2 * channels), F32),
            shape((pair_rows, 2 * channels), F32),
            shape((pair_rows, 2 * channels), F32),
            shape((3 * rows + extra, cols), jnp.int16),
        ),
        in_specs=[scalar] * 2 + [one] * 8,
        out_specs=[one] * 5,
        compiler_params=params,
        cost_estimate=pl.CostEstimate(flops=30000000, bytes_accessed=5000000, transcendentals=0),
    )(place, timesteps, states[0], noise_draws[0], out_gate, embed_weight, context, qkv_weight, out_weight.T, head_weight)
    gathered = lax.all_to_all(payload, "seq", 0, 0).reshape(tokens, reach + 128)
    chunks = lax.all_gather(chunk, "tm")
    flipped = lax.ppermute(gathered, "tm", flip)

    def fixed(*dims):
        return pl.BlockSpec(dims, lambda i, place: (0,) * len(dims))

    def halved(body, at, more_in, out_shape, out_specs, scratch, flops):
        return pl.pallas_call(
            body,
            out_shape=out_shape,
            grid_spec=pltpu.PrefetchScalarGridSpec(
                num_scalar_prefetch=1,
                grid=(3,),
                in_specs=[
                    fixed(tokens, reach),
                    pl.BlockSpec((channels, reach), lambda i, place: (0, at(place[0]))),
                    pl.BlockSpec((2, reach), lambda i, place: (0, at(place[0]))),
                    pl.BlockSpec((chips, rows, cols), lambda i, place: (at(place[0]), i, 0)),
                    pl.BlockSpec((chips, extra, cols), lambda i, place: (at(place[0]), 3 * rows // extra, 0)),
                ]
                + more_in,
                out_specs=out_specs,
                scratch_shapes=[pltpu.VMEM((half, reach), BF16), pltpu.VMEM((reach, cols), BF16)] + scratch,
            ),
            compiler_params=pltpu.CompilerParams(vmem_limit_bytes=46 * 1024 * 1024),
            cost_estimate=pl.CostEstimate(flops=flops, bytes_accessed=9000000, transcendentals=0),
        )

    by_kind = pl.BlockSpec((half, cols), lambda i, place: (i, 0))
    sums, heads = halved(
        first_half,
        lambda c: c,
        [],
        (shape((3 * half, cols), F32), shape((channels, cols), F32)),
        [by_kind, fixed(channels, cols)],
        [],
        100000000000,
    )(place, gathered, embed_weight, modulation[0], chunks, chunks)
    shares = halved(
        second_half,
        lambda c: 1 - c,
        [by_kind, fixed(channels, cols), pl.BlockSpec((tokens, 128), lambda i, place: (0, reach // 128))],
        shape((peers, pair_rows, 2 * channels), BF16),
        fixed(peers, pair_rows, 2 * channels),
        [pltpu.VMEM((3, tokens, cols), BF16)],
        4000000000,
    )(place, flipped, embed_weight, modulation[0], chunks, chunks, sums, heads, gathered)
    shares = lax.all_to_all(shares, "seq", 0, 0)
    mixed = jnp.sum(shares.astype(F32), axis=0)

    def unpairs(value):
        return jnp.concatenate([value[:, :channels], value[:, channels:]], axis=0)

    velocity_f = gains * mixed
    drift = sizes * velocity_f + kicks
    both = lax.all_gather(drift, "tm", axis_index_groups=[[2 * i, 2 * i + 1] for i in range(chips)])
    spread = jnp.broadcast_to((both[0] + both[1]).astype(BF16)[None], (chips, pair_rows, 2 * channels))
    everyone = lax.all_to_all(spread, "tm", 0, 0, axis_index_groups=same_core).astype(F32)
    earlier = lax.broadcasted_iota(jnp.int32, (chips, 1, 1), 0) < z
    before = jnp.sum(jnp.where(earlier, everyone, 0.0), axis=0) + jnp.where(core == 1, both[0], 0.0)
    new_states = initial + unpairs(before)
    return (new_states[None], unpairs(velocity_f).astype(BF16)[None])


def solution(mesh):
    in_specs = (
        P("tm", "seq", None),
        P("seq", None),
        P("tm", "seq", None),
        P("tm", None),
        P("seq", None),
        P("tm", None, None),
        P("tm", None),
        P(),
        P(None, "tm", "seq"),
        P("seq", "tm"),
        P(None, "tm"),
    )
    out_specs = (P("tm", "seq", None), P("tm", "seq", None))
    return jax.shard_map(per_device, mesh=mesh, in_specs=in_specs, out_specs=out_specs, check_vma=False)
```

```python
import math

import jax
import jax.numpy as jnp
from jax import lax
from jax.experimental import pallas as pl
from jax.experimental.pallas import tpu as pltpu
from jax.sharding import PartitionSpec as P

HEAD = 128
NT = 1000
F32 = jnp.float32
BF16 = jnp.bfloat16
KEPT = 14.0
LIMIT = 56 * 1024 * 1024


def sigma_of(level_ids):
    fraction = (level_ids.astype(F32) + 1.0) / NT
    return 5.0 * fraction / (1.0 + 4.0 * fraction)


def dot_nt(a, b):
    return lax.dot_general(a, b, (((1,), (1,)), ((), ())), preferred_element_type=F32)


def dot_nn(a, b):
    return lax.dot_general(a, b, (((1,), (0,)), ((), ())), preferred_element_type=F32)


def split_two(value):
    high = value.astype(BF16)
    return high, (value - high.astype(F32)).astype(BF16)


def to_whole(weight):
    peak = jnp.maximum(jnp.max(jnp.abs(weight), axis=0, keepdims=True), 1e-30)
    power = jnp.floor(-jnp.log2(peak))
    whole = jnp.round(weight * jnp.exp2(power + KEPT))
    return whole.astype(jnp.int32).astype(jnp.int16), power


def from_whole(whole, power):
    return whole.astype(F32) * jnp.exp2(-(power + KEPT))


def pack_weights(qkv_ref, out_ref, head_ref, chunk_ref):
    count, rows, cols = qkv_ref.shape
    channels = head_ref.shape[0]
    row = lax.broadcasted_iota(jnp.int32, (16, cols), 0)
    meta = jnp.zeros((16, cols), F32)
    for i in range(count):
        chunk_ref[i * rows : (i + 1) * rows, :], power = to_whole(qkv_ref[i].astype(F32))
        meta = jnp.where(row == i, power, meta)
    at = count * rows
    chunk_ref[at : at + channels, :], power = to_whole(dot_nn(head_ref[...], out_ref[...]))
    meta = jnp.where(row == count, power, meta)
    chunk_ref[at + channels :, :] = meta.astype(jnp.int32).astype(jnp.int16)


def pack(core_ref, times_ref, states_ref, noise_ref, gate_ref, embed_ref, context_ref, *refs):
    weight_refs, (payload_ref, gains_ref, sizes_ref, kicks_ref, chunk_ref) = refs[:3], refs[3:]
    peers, tokens, lanes = payload_ref.shape
    channels = embed_ref.shape[0]
    half = lanes - 128
    here = pl.ds(pl.multiple_of(core_ref[0] * half, 128), half)
    latent = states_ref[...].astype(BF16)
    payload_ref[0, :, :half] = context_ref[:, here]
    hidden = dot_nn(latent, embed_ref[...]) + context_ref[...].astype(F32)
    scale = lax.rsqrt(jnp.mean(hidden * hidden, axis=-1, keepdims=True) + 1e-06)
    high, low = split_two(scale)
    lane = lax.broadcasted_iota(jnp.int32, (tokens, 128), 1)
    tail = jnp.concatenate([latent.astype(F32), jnp.zeros((tokens, 128 - channels), F32)], axis=1)
    tail = jnp.where(lane == channels, high.astype(F32), tail)
    tail = jnp.where(lane == channels + 1, low.astype(F32), tail)
    payload_ref[0, :, half:] = tail.astype(BF16)
    for p in range(1, peers):
        payload_ref[p] = payload_ref[0]
    gain = 1.0 + jnp.concatenate([gate_ref[...], gate_ref[...]], axis=1)
    now = jnp.full(gain.shape, times_ref[0, 0], jnp.int32)
    later = jnp.full(gain.shape, times_ref[0, 1], jnp.int32)
    step_size = sigma_of(later) - sigma_of(now)
    gains_ref[...] = jnp.broadcast_to(gain, gains_ref.shape)
    sizes_ref[...] = jnp.broadcast_to(step_size, sizes_ref.shape)
    pair_rows = tokens // 2
    noise = jnp.concatenate([noise_ref[:pair_rows], noise_ref[pair_rows:]], axis=1)
    kicks_ref[...] = jnp.sqrt(-step_size) * noise
    pack_weights(*weight_refs, chunk_ref)


def scale_rows(left_ref, context_ref, embed_ref, mods_ref):
    tokens, channels = context_ref.shape[0], embed_ref.shape[0]
    gain = 1.0 + mods_ref[1:2, :]
    short = gain.astype(BF16)
    left_ref[:tokens, :] = context_ref[...] * short
    left_ref[tokens : tokens + channels, :] = embed_ref[...] * short
    row = lax.broadcasted_iota(jnp.int32, (16, gain.shape[1]), 0)
    left_ref[tokens + channels :, :] = jnp.where(row == 0, mods_ref[0:1, :], 0.0).astype(BF16)


def product(i, chunk_ref, extra_ref, left_ref, weight_ref):
    chips, rows, cols = chunk_ref.shape
    row = lax.broadcasted_iota(jnp.int32, (16, cols), 0)
    for n in range(chips):
        meta = extra_ref[n, extra_ref.shape[1] - 16 :, :].astype(F32)
        power = jnp.sum(jnp.where(row == i, meta, 0.0), axis=0, keepdims=True)
        weight_ref[n * rows : (n + 1) * rows, :] = chunk_ref[n].astype(BF16) * jnp.exp2(-(power + KEPT)).astype(BF16)
    return dot_nn(left_ref[...], weight_ref[...])


def head_shares(extra_ref):
    channels = extra_ref.shape[1] - 16
    heads = None
    for n in range(extra_ref.shape[0]):
        power = extra_ref[n, channels:, :].astype(F32)[3:4]
        share = from_whole(extra_ref[n, :channels, :], power)
        heads = share if heads is None else heads + share
    return heads


def first_half(
    place_ref, context_ref, embed_ref, mods_ref, chunk_ref, extra_ref, sums_ref, heads_ref, left_ref, weight_ref
):
    i = pl.program_id(0)

    @pl.when(i == 0)
    def _():
        scale_rows(left_ref, context_ref, embed_ref, mods_ref)
        heads_ref[...] = head_shares(extra_ref)

    sums_ref[...] = product(i, chunk_ref, extra_ref, left_ref, weight_ref)


def second_half(
    place_ref,
    context_ref,
    embed_ref,
    mods_ref,
    chunk_ref,
    extra_ref,
    sums_ref,
    heads_ref,
    tail_ref,
    out_ref,
    left_ref,
    weight_ref,
    made_ref,
):
    i = pl.program_id(0)
    tokens, channels = context_ref.shape[0], embed_ref.shape[0]

    @pl.when(i == 0)
    def _():
        scale_rows(left_ref, context_ref, embed_ref, mods_ref)

    total = sums_ref[...] + product(i, chunk_ref, extra_ref, left_ref, weight_ref)
    latent = tail_ref[:, :channels]
    scale = tail_ref[:, channels : channels + 1].astype(F32) + tail_ref[:, channels + 1 : channels + 2].astype(F32)
    high, low = split_two(total[tokens : tokens + channels])
    body = total[:tokens] + dot_nn(latent, high) + dot_nn(latent, low)
    made_ref[i] = (body * scale + total[tokens + channels : tokens + channels + 1]).astype(BF16)

    @pl.when(i == pl.num_programs(0) - 1)
    def _():
        outs = []
        for h in range(made_ref.shape[2] // HEAD):
            cols = slice(h * HEAD, (h + 1) * HEAD)
            scores = dot_nt(made_ref[0, :, cols], made_ref[1, :, cols]) * (math.log2(math.e) / math.sqrt(HEAD))
            weights = jnp.exp2(scores - jnp.max(scores, axis=-1, keepdims=True)).astype(BF16)
            values = made_ref[2, :, cols]
            mixed = dot_nn(weights, jnp.concatenate([values, jnp.ones_like(values)], axis=1))
            outs.append((mixed[:, :HEAD] / mixed[:, HEAD:]).astype(BF16))
        attended = jnp.concatenate(outs, axis=1)
        head_high, head_low = split_two(heads_ref[...] + head_shares(extra_ref))
        result = dot_nt(attended, head_high) + dot_nt(attended, head_low)
        peers, pair_rows, _ = out_ref.shape
        for p in range(peers):
            at = 2 * p * pair_rows
            block = jnp.concatenate([result[at : at + pair_rows], result[at + pair_rows : at + 2 * pair_rows]], axis=1)
            out_ref[p] = block.astype(BF16)


def per_device(
    states, initial, noise_draws, timesteps, context, modulation, out_gate, embed_weight, qkv_weight, out_weight, head_weight
):
    steps, peers = lax.axis_size("tm"), lax.axis_size("seq")
    chips = steps // 2
    mine = lax.axis_index("tm")
    z, core = mine >> 1, mine & 1
    tokens_here, channels = initial.shape
    rows, cols = qkv_weight.shape[1:]
    tokens = tokens_here * peers
    half = tokens + channels + 16
    reach = chips * rows
    extra = channels + 16
    shape = jax.ShapeDtypeStruct
    place = core[None]

    flip = [(i, i ^ 1) for i in range(steps)]
    same_core = [list(range(0, steps, 2)), list(range(1, steps, 2))]
    one = pl.BlockSpec(memory_space=pltpu.VMEM)
    scalar = pl.BlockSpec(memory_space=pltpu.SMEM)
    params = pltpu.CompilerParams(vmem_limit_bytes=LIMIT)

    pair_rows = tokens_here // 2
    payload, gains, sizes, kicks, chunk = pl.pallas_call(
        pack,
        out_shape=(
            shape((peers, tokens_here, reach + 128), BF16),
            shape((pair_rows, 2 * channels), F32),
            shape((pair_rows, 2 * channels), F32),
            shape((pair_rows, 2 * channels), F32),
            shape((3 * rows + extra, cols), jnp.int16),
        ),
        in_specs=[scalar] * 2 + [one] * 8,
        out_specs=[one] * 5,
        compiler_params=params,
        cost_estimate=pl.CostEstimate(flops=30000000, bytes_accessed=5000000, transcendentals=0),
    )(place, timesteps, states[0], noise_draws[0], out_gate, embed_weight, context, qkv_weight, out_weight.T, head_weight)
    gathered = lax.all_to_all(payload, "seq", 0, 0).reshape(tokens, reach + 128)
    chunks = lax.all_gather(chunk, "tm")
    flipped = lax.ppermute(gathered, "tm", flip)

    def fixed(*dims):
        return pl.BlockSpec(dims, lambda i, place: (0,) * len(dims))

    def halved(body, at, more_in, out_shape, out_specs, scratch, flops):
        return pl.pallas_call(
            body,
            out_shape=out_shape,
            grid_spec=pltpu.PrefetchScalarGridSpec(
                num_scalar_prefetch=1,
                grid=(3,),
                in_specs=[
                    fixed(tokens, reach),
                    pl.BlockSpec((channels, reach), lambda i, place: (0, at(place[0]))),
                    pl.BlockSpec((2, reach), lambda i, place: (0, at(place[0]))),
                    pl.BlockSpec((chips, rows, cols), lambda i, place: (at(place[0]), i, 0)),
                    pl.BlockSpec((chips, extra, cols), lambda i, place: (at(place[0]), 3 * rows // extra, 0)),
                ]
                + more_in,
                out_specs=out_specs,
                scratch_shapes=[pltpu.VMEM((half, reach), BF16), pltpu.VMEM((reach, cols), BF16)] + scratch,
            ),
            compiler_params=pltpu.CompilerParams(vmem_limit_bytes=46 * 1024 * 1024),
            cost_estimate=pl.CostEstimate(flops=flops, bytes_accessed=9000000, transcendentals=0),
        )

    by_kind = pl.BlockSpec((half, cols), lambda i, place: (i, 0))
    sums, heads = halved(
        first_half,
        lambda c: c,
        [],
        (shape((3 * half, cols), F32), shape((channels, cols), F32)),
        [by_kind, fixed(channels, cols)],
        [],
        100000000000,
    )(place, gathered, embed_weight, modulation[0], chunks, chunks)
    shares = halved(
        second_half,
        lambda c: 1 - c,
        [by_kind, fixed(channels, cols), pl.BlockSpec((tokens, 128), lambda i, place: (0, reach // 128))],
        shape((peers, pair_rows, 2 * channels), BF16),
        fixed(peers, pair_rows, 2 * channels),
        [pltpu.VMEM((3, tokens, cols), BF16)],
        4000000000,
    )(place, flipped, embed_weight, modulation[0], chunks, chunks, sums, heads, gathered)
    shares = lax.all_to_all(shares, "seq", 0, 0)
    mixed = jnp.sum(shares.astype(F32), axis=0)

    def unpairs(value):
        return jnp.concatenate([value[:, :channels], value[:, channels:]], axis=0)

    velocity_f = gains * mixed
    drift = sizes * velocity_f + kicks
    both = lax.all_gather(drift, "tm", axis_index_groups=[[2 * i, 2 * i + 1] for i in range(chips)])
    spread = jnp.broadcast_to((both[0] + both[1]).astype(BF16)[None], (chips, pair_rows, 2 * channels))
    everyone = lax.all_to_all(spread, "tm", 0, 0, axis_index_groups=same_core).astype(F32)
    earlier = lax.broadcasted_iota(jnp.int32, (chips, 1, 1), 0) < z
    before = jnp.sum(jnp.where(earlier, everyone, 0.0), axis=0) + jnp.where(core == 1, both[0], 0.0)
    new_states = initial + unpairs(before)
    return (new_states[None], unpairs(velocity_f).astype(BF16)[None])


def solution(mesh):
    in_specs = (
        P("tm", "seq", None),
        P("seq", None),
        P("tm", "seq", None),
        P("tm", None),
        P("seq", None),
        P("tm", None, None),
        P("tm", None),
        P(),
        P(None, "tm", "seq"),
        P("seq", "tm"),
        P(None, "tm"),
    )
    out_specs = (P("tm", "seq", None), P("tm", "seq", None))
    return jax.shard_map(per_device, mesh=mesh, in_specs=in_specs, out_specs=out_specs, check_vma=False)
```

```python
import math

import jax
import jax.numpy as jnp
from jax import lax
from jax.experimental import pallas as pl
from jax.experimental.pallas import tpu as pltpu
from jax.sharding import PartitionSpec as P

HEAD = 128
NT = 1000
F32 = jnp.float32
BF16 = jnp.bfloat16
KEPT = 14.0
LIMIT = 56 * 1024 * 1024


def sigma_of(level_ids):
    fraction = (level_ids.astype(F32) + 1.0) / NT
    return 5.0 * fraction / (1.0 + 4.0 * fraction)


def dot_nt(a, b):
    return lax.dot_general(a, b, (((1,), (1,)), ((), ())), preferred_element_type=F32)


def dot_nn(a, b):
    return lax.dot_general(a, b, (((1,), (0,)), ((), ())), preferred_element_type=F32)


def split_two(value):
    high = value.astype(BF16)
    return high, (value - high.astype(F32)).astype(BF16)


def to_whole(weight):
    peak = jnp.maximum(jnp.max(jnp.abs(weight), axis=0, keepdims=True), 1e-30)
    power = jnp.floor(-jnp.log2(peak))
    whole = jnp.round(weight * jnp.exp2(power + KEPT))
    return whole.astype(jnp.int32).astype(jnp.int16), power


def from_whole(whole, power):
    return whole.astype(F32) * jnp.exp2(-(power + KEPT))


def pack_weights(qkv_ref, out_ref, head_ref, chunk_ref):
    count, rows, cols = qkv_ref.shape
    channels = head_ref.shape[0]
    row = lax.broadcasted_iota(jnp.int32, (16, cols), 0)
    meta = jnp.zeros((16, cols), F32)
    for i in range(count):
        chunk_ref[i * rows : (i + 1) * rows, :], power = to_whole(qkv_ref[i].astype(F32))
        meta = jnp.where(row == i, power, meta)
    at = count * rows
    chunk_ref[at : at + channels, :], power = to_whole(dot_nn(head_ref[...], out_ref[...]))
    meta = jnp.where(row == count, power, meta)
    chunk_ref[at + channels :, :] = meta.astype(jnp.int32).astype(jnp.int16)


def pack(core_ref, times_ref, states_ref, noise_ref, gate_ref, embed_ref, context_ref, *refs):
    weight_refs, (payload_ref, gains_ref, sizes_ref, kicks_ref, chunk_ref) = refs[:3], refs[3:]
    peers, tokens, lanes = payload_ref.shape
    channels = embed_ref.shape[0]
    half = lanes - 128
    here = pl.ds(pl.multiple_of(core_ref[0] * half, 128), half)
    latent = states_ref[...].astype(BF16)
    payload_ref[0, :, :half] = context_ref[:, here]
    hidden = dot_nn(latent, embed_ref[...]) + context_ref[...].astype(F32)
    scale = lax.rsqrt(jnp.mean(hidden * hidden, axis=-1, keepdims=True) + 1e-06)
    high, low = split_two(scale)
    lane = lax.broadcasted_iota(jnp.int32, (tokens, 128), 1)
    tail = jnp.concatenate([latent.astype(F32), jnp.zeros((tokens, 128 - channels), F32)], axis=1)
    tail = jnp.where(lane == channels, high.astype(F32), tail)
    tail = jnp.where(lane == channels + 1, low.astype(F32), tail)
    payload_ref[0, :, half:] = tail.astype(BF16)
    for p in range(1, peers):
        payload_ref[p] = payload_ref[0]
    gain = 1.0 + jnp.concatenate([gate_ref[...], gate_ref[...]], axis=1)
    now = jnp.full(gain.shape, times_ref[0, 0], jnp.int32)
    later = jnp.full(gain.shape, times_ref[0, 1], jnp.int32)
    step_size = sigma_of(later) - sigma_of(now)
    gains_ref[...] = jnp.broadcast_to(gain, gains_ref.shape)
    sizes_ref[...] = jnp.broadcast_to(step_size, sizes_ref.shape)
    pair_rows = tokens // 2
    noise = jnp.concatenate([noise_ref[:pair_rows], noise_ref[pair_rows:]], axis=1)
    kicks_ref[...] = jnp.sqrt(-step_size) * noise
    pack_weights(*weight_refs, chunk_ref)


def scale_rows(left_ref, context_ref, embed_ref, mods_ref):
    tokens, channels = context_ref.shape[0], embed_ref.shape[0]
    gain = 1.0 + mods_ref[1:2, :]
    short = gain.astype(BF16)
    left_ref[:tokens, :] = context_ref[...] * short
    left_ref[tokens : tokens + channels, :] = embed_ref[...] * short
    row = lax.broadcasted_iota(jnp.int32, (16, gain.shape[1]), 0)
    left_ref[tokens + channels :, :] = jnp.where(row == 0, mods_ref[0:1, :], 0.0).astype(BF16)


def product(i, chunk_ref, extra_ref, left_ref, weight_ref):
    chips, rows, cols = chunk_ref.shape
    row = lax.broadcasted_iota(jnp.int32, (16, cols), 0)
    for n in range(chips):
        meta = extra_ref[n, extra_ref.shape[1] - 16 :, :].astype(F32)
        power = jnp.sum(jnp.where(row == i, meta, 0.0), axis=0, keepdims=True)
        weight_ref[n * rows : (n + 1) * rows, :] = chunk_ref[n].astype(BF16) * jnp.exp2(-(power + KEPT)).astype(BF16)
    return dot_nn(left_ref[...], weight_ref[...])


def head_shares(extra_ref):
    channels = extra_ref.shape[1] - 16
    heads = None
    for n in range(extra_ref.shape[0]):
        power = extra_ref[n, channels:, :].astype(F32)[3:4]
        share = from_whole(extra_ref[n, :channels, :], power)
        heads = share if heads is None else heads + share
    return heads


def first_half(
    place_ref, context_ref, embed_ref, mods_ref, chunk_ref, extra_ref, sums_ref, heads_ref, left_ref, weight_ref
):
    i = pl.program_id(0)

    @pl.when(i == 0)
    def _():
        scale_rows(left_ref, context_ref, embed_ref, mods_ref)
        heads_ref[...] = head_shares(extra_ref)

    sums_ref[...] = product(i, chunk_ref, extra_ref, left_ref, weight_ref)


def second_half(
    place_ref,
    context_ref,
    embed_ref,
    mods_ref,
    chunk_ref,
    extra_ref,
    sums_ref,
    heads_ref,
    tail_ref,
    out_ref,
    left_ref,
    weight_ref,
    made_ref,
):
    i = pl.program_id(0)
    tokens, channels = context_ref.shape[0], embed_ref.shape[0]

    @pl.when(i == 0)
    def _():
        scale_rows(left_ref, context_ref, embed_ref, mods_ref)

    total = sums_ref[...] + product(i, chunk_ref, extra_ref, left_ref, weight_ref)
    latent = tail_ref[:, :channels]
    scale = tail_ref[:, channels : channels + 1].astype(F32) + tail_ref[:, channels + 1 : channels + 2].astype(F32)
    high, low = split_two(total[tokens : tokens + channels])
    body = total[:tokens] + dot_nn(latent, high) + dot_nn(latent, low)
    made_ref[i] = (body * scale + total[tokens + channels : tokens + channels + 1]).astype(BF16)

    @pl.when(i == pl.num_programs(0) - 1)
    def _():
        outs = []
        for h in range(made_ref.shape[2] // HEAD):
            cols = slice(h * HEAD, (h + 1) * HEAD)
            scores = dot_nt(made_ref[0, :, cols], made_ref[1, :, cols]) * (math.log2(math.e) / math.sqrt(HEAD))
            weights = jnp.exp2(scores - jnp.max(scores, axis=-1, keepdims=True)).astype(BF16)
            values = made_ref[2, :, cols]
            mixed = dot_nn(weights, jnp.concatenate([values, jnp.ones_like(values)], axis=1))
            outs.append((mixed[:, :HEAD] / mixed[:, HEAD:]).astype(BF16))
        attended = jnp.concatenate(outs, axis=1)
        head_high, head_low = split_two(heads_ref[...] + head_shares(extra_ref))
        result = dot_nt(attended, head_high) + dot_nt(attended, head_low)
        peers, pair_rows, _ = out_ref.shape
        for p in range(peers):
            at = 2 * p * pair_rows
            block = jnp.concatenate([result[at : at + pair_rows], result[at + pair_rows : at + 2 * pair_rows]], axis=1)
            out_ref[p] = block.astype(BF16)


def spread_sum(both_ref, out_ref):
    out_ref[...] = jnp.broadcast_to((both_ref[0] + both_ref[1]).astype(BF16)[None], out_ref.shape)


def per_device(
    states, initial, noise_draws, timesteps, context, modulation, out_gate, embed_weight, qkv_weight, out_weight, head_weight
):
    steps, peers = lax.axis_size("tm"), lax.axis_size("seq")
    chips = steps // 2
    mine = lax.axis_index("tm")
    z, core = mine >> 1, mine & 1
    tokens_here, channels = initial.shape
    rows, cols = qkv_weight.shape[1:]
    tokens = tokens_here * peers
    half = tokens + channels + 16
    reach = chips * rows
    extra = channels + 16
    shape = jax.ShapeDtypeStruct
    place = core[None]

    flip = [(i, i ^ 1) for i in range(steps)]
    same_core = [list(range(0, steps, 2)), list(range(1, steps, 2))]
    one = pl.BlockSpec(memory_space=pltpu.VMEM)
    scalar = pl.BlockSpec(memory_space=pltpu.SMEM)
    params = pltpu.CompilerParams(vmem_limit_bytes=LIMIT)

    pair_rows = tokens_here // 2
    payload, gains, sizes, kicks, chunk = pl.pallas_call(
        pack,
        out_shape=(
            shape((peers, tokens_here, reach + 128), BF16),
            shape((pair_rows, 2 * channels), F32),
            shape((pair_rows, 2 * channels), F32),
            shape((pair_rows, 2 * channels), F32),
            shape((3 * rows + extra, cols), jnp.int16),
        ),
        in_specs=[scalar] * 2 + [one] * 8,
        out_specs=[one] * 5,
        compiler_params=params,
        cost_estimate=pl.CostEstimate(flops=30000000, bytes_accessed=5000000, transcendentals=0),
    )(place, timesteps, states[0], noise_draws[0], out_gate, embed_weight, context, qkv_weight, out_weight.T, head_weight)
    gathered = lax.all_to_all(payload, "seq", 0, 0).reshape(tokens, reach + 128)
    chunks = lax.all_gather(chunk, "tm")
    flipped = lax.ppermute(gathered, "tm", flip)

    def fixed(*dims):
        return pl.BlockSpec(dims, lambda i, place: (0,) * len(dims))

    def halved(body, at, more_in, out_shape, out_specs, scratch, flops):
        return pl.pallas_call(
            body,
            out_shape=out_shape,
            grid_spec=pltpu.PrefetchScalarGridSpec(
                num_scalar_prefetch=1,
                grid=(3,),
                in_specs=[
                    fixed(tokens, reach),
                    pl.BlockSpec((channels, reach), lambda i, place: (0, at(place[0]))),
                    pl.BlockSpec((2, reach), lambda i, place: (0, at(place[0]))),
                    pl.BlockSpec((chips, rows, cols), lambda i, place: (at(place[0]), i, 0)),
                    pl.BlockSpec((chips, extra, cols), lambda i, place: (at(place[0]), 3 * rows // extra, 0)),
                ]
                + more_in,
                out_specs=out_specs,
                scratch_shapes=[pltpu.VMEM((half, reach), BF16), pltpu.VMEM((reach, cols), BF16)] + scratch,
            ),
            compiler_params=pltpu.CompilerParams(vmem_limit_bytes=46 * 1024 * 1024),
            cost_estimate=pl.CostEstimate(flops=flops, bytes_accessed=9000000, transcendentals=0),
        )

    by_kind = pl.BlockSpec((half, cols), lambda i, place: (i, 0))
    sums, heads = halved(
        first_half,
        lambda c: c,
        [],
        (shape((3 * half, cols), F32), shape((channels, cols), F32)),
        [by_kind, fixed(channels, cols)],
        [],
        100000000000,
    )(place, gathered, embed_weight, modulation[0], chunks, chunks)
    shares = halved(
        second_half,
        lambda c: 1 - c,
        [by_kind, fixed(channels, cols), pl.BlockSpec((tokens, 128), lambda i, place: (0, reach // 128))],
        shape((peers, pair_rows, 2 * channels), BF16),
        fixed(peers, pair_rows, 2 * channels),
        [pltpu.VMEM((3, tokens, cols), BF16)],
        4000000000,
    )(place, flipped, embed_weight, modulation[0], chunks, chunks, sums, heads, gathered)
    shares = lax.all_to_all(shares, "seq", 0, 0)
    mixed = jnp.sum(shares.astype(F32), axis=0)

    def unpairs(value):
        return jnp.concatenate([value[:, :channels], value[:, channels:]], axis=0)

    velocity_f = gains * mixed
    drift = sizes * velocity_f + kicks
    both = lax.all_gather(drift, "tm", axis_index_groups=[[2 * i, 2 * i + 1] for i in range(chips)])
    spread = pl.pallas_call(
        spread_sum,
        out_shape=shape((chips, pair_rows, 2 * channels), BF16),
        in_specs=[one],
        out_specs=one,
        compiler_params=pltpu.CompilerParams(vmem_limit_bytes=8 * 1024 * 1024),
    )(both)
    everyone = lax.all_to_all(spread, "tm", 0, 0, axis_index_groups=same_core).astype(F32)
    earlier = lax.broadcasted_iota(jnp.int32, (chips, 1, 1), 0) < z
    before = jnp.sum(jnp.where(earlier, everyone, 0.0), axis=0) + jnp.where(core == 1, both[0], 0.0)
    new_states = initial + unpairs(before)
    return (new_states[None], unpairs(velocity_f).astype(BF16)[None])


def solution(mesh):
    in_specs = (
        P("tm", "seq", None),
        P("seq", None),
        P("tm", "seq", None),
        P("tm", None),
        P("seq", None),
        P("tm", None, None),
        P("tm", None),
        P(),
        P(None, "tm", "seq"),
        P("seq", "tm"),
        P(None, "tm"),
    )
    out_specs = (P("tm", "seq", None), P("tm", "seq", None))
    return jax.shard_map(per_device, mesh=mesh, in_specs=in_specs, out_specs=out_specs, check_vma=False)
```

```python
import math

import jax
import jax.numpy as jnp
from jax import lax
from jax.experimental import pallas as pl
from jax.experimental.pallas import tpu as pltpu
from jax.sharding import PartitionSpec as P

HEAD = 128
NT = 1000
F32 = jnp.float32
BF16 = jnp.bfloat16
KEPT = 14.0
LIMIT = 56 * 1024 * 1024


def sigma_of(level_ids):
    fraction = (level_ids.astype(F32) + 1.0) / NT
    return 5.0 * fraction / (1.0 + 4.0 * fraction)


def dot_nt(a, b):
    return lax.dot_general(a, b, (((1,), (1,)), ((), ())), preferred_element_type=F32)


def dot_nn(a, b):
    return lax.dot_general(a, b, (((1,), (0,)), ((), ())), preferred_element_type=F32)


def split_two(value):
    high = value.astype(BF16)
    return high, (value - high.astype(F32)).astype(BF16)


def to_whole(weight):
    peak = jnp.maximum(jnp.max(jnp.abs(weight), axis=0, keepdims=True), 1e-30)
    power = jnp.floor(-jnp.log2(peak))
    whole = jnp.round(weight * jnp.exp2(power + KEPT))
    return whole.astype(jnp.int32).astype(jnp.int16), power


def from_whole(whole, power):
    return whole.astype(F32) * jnp.exp2(-(power + KEPT))


def pack_weights(qkv_ref, out_ref, head_ref, chunk_ref):
    count, rows, cols = qkv_ref.shape
    channels = head_ref.shape[0]
    row = lax.broadcasted_iota(jnp.int32, (16, cols), 0)
    meta = jnp.zeros((16, cols), F32)
    for i in range(count):
        chunk_ref[i * rows : (i + 1) * rows, :], power = to_whole(qkv_ref[i].astype(F32))
        meta = jnp.where(row == i, power, meta)
    at = count * rows
    chunk_ref[at : at + channels, :], power = to_whole(dot_nn(head_ref[...], out_ref[...]))
    meta = jnp.where(row == count, power, meta)
    chunk_ref[at + channels :, :] = meta.astype(jnp.int32).astype(jnp.int16)


def pack(core_ref, times_ref, states_ref, noise_ref, gate_ref, embed_ref, context_ref, *refs):
    weight_refs, (payload_ref, gains_ref, sizes_ref, kicks_ref, chunk_ref) = refs[:3], refs[3:]
    peers, tokens, lanes = payload_ref.shape
    channels = embed_ref.shape[0]
    half = lanes - 128
    here = pl.ds(pl.multiple_of(core_ref[0] * half, 128), half)
    latent = states_ref[...].astype(BF16)
    payload_ref[0, :, :half] = context_ref[:, here]
    hidden = dot_nn(latent, embed_ref[...]) + context_ref[...].astype(F32)
    scale = lax.rsqrt(jnp.mean(hidden * hidden, axis=-1, keepdims=True) + 1e-06)
    high, low = split_two(scale)
    lane = lax.broadcasted_iota(jnp.int32, (tokens, 128), 1)
    tail = jnp.concatenate([latent.astype(F32), jnp.zeros((tokens, 128 - channels), F32)], axis=1)
    tail = jnp.where(lane == channels, high.astype(F32), tail)
    tail = jnp.where(lane == channels + 1, low.astype(F32), tail)
    payload_ref[0, :, half:] = tail.astype(BF16)
    for p in range(1, peers):
        payload_ref[p] = payload_ref[0]
    gain = 1.0 + jnp.concatenate([gate_ref[...], gate_ref[...]], axis=1)
    now = jnp.full(gain.shape, times_ref[0, 0], jnp.int32)
    later = jnp.full(gain.shape, times_ref[0, 1], jnp.int32)
    step_size = sigma_of(later) - sigma_of(now)
    gains_ref[...] = jnp.broadcast_to(gain, gains_ref.shape)
    sizes_ref[...] = jnp.broadcast_to(step_size, sizes_ref.shape)
    pair_rows = tokens // 2
    noise = jnp.concatenate([noise_ref[:pair_rows], noise_ref[pair_rows:]], axis=1)
    kicks_ref[...] = jnp.sqrt(-step_size) * noise
    pack_weights(*weight_refs, chunk_ref)


def scale_rows(left_ref, context_ref, embed_ref, mods_ref):
    tokens, channels = context_ref.shape[0], embed_ref.shape[0]
    gain = 1.0 + mods_ref[1:2, :]
    short = gain.astype(BF16)
    left_ref[:tokens, :] = context_ref[...] * short
    left_ref[tokens : tokens + channels, :] = embed_ref[...] * short
    row = lax.broadcasted_iota(jnp.int32, (16, gain.shape[1]), 0)
    left_ref[tokens + channels :, :] = jnp.where(row == 0, mods_ref[0:1, :], 0.0).astype(BF16)


def product(i, chunk_ref, extra_ref, left_ref, weight_ref):
    chips, rows, cols = chunk_ref.shape
    row = lax.broadcasted_iota(jnp.int32, (16, cols), 0)
    for n in range(chips):
        meta = extra_ref[n, extra_ref.shape[1] - 16 :, :].astype(F32)
        power = jnp.sum(jnp.where(row == i, meta, 0.0), axis=0, keepdims=True)
        weight_ref[n * rows : (n + 1) * rows, :] = chunk_ref[n].astype(BF16) * jnp.exp2(-(power + KEPT)).astype(BF16)
    return dot_nn(left_ref[...], weight_ref[...])


def head_shares(extra_ref):
    channels = extra_ref.shape[1] - 16
    heads = None
    for n in range(extra_ref.shape[0]):
        power = extra_ref[n, channels:, :].astype(F32)[3:4]
        share = from_whole(extra_ref[n, :channels, :], power)
        heads = share if heads is None else heads + share
    return heads


def first_half(
    place_ref, context_ref, embed_ref, mods_ref, chunk_ref, extra_ref, sums_ref, heads_ref, left_ref, weight_ref
):
    i = pl.program_id(0)

    @pl.when(i == 0)
    def _():
        scale_rows(left_ref, context_ref, embed_ref, mods_ref)
        heads_ref[...] = head_shares(extra_ref)

    sums_ref[...] = product(i, chunk_ref, extra_ref, left_ref, weight_ref)


def second_half(
    place_ref,
    context_ref,
    embed_ref,
    mods_ref,
    chunk_ref,
    extra_ref,
    sums_ref,
    heads_ref,
    tail_ref,
    out_ref,
    left_ref,
    weight_ref,
    made_ref,
):
    i = pl.program_id(0)
    tokens, channels = context_ref.shape[0], embed_ref.shape[0]

    @pl.when(i == 0)
    def _():
        scale_rows(left_ref, context_ref, embed_ref, mods_ref)

    total = sums_ref[...] + product(i, chunk_ref, extra_ref, left_ref, weight_ref)
    latent = tail_ref[:, :channels]
    scale = tail_ref[:, channels : channels + 1].astype(F32) + tail_ref[:, channels + 1 : channels + 2].astype(F32)
    high, low = split_two(total[tokens : tokens + channels])
    body = total[:tokens] + dot_nn(latent, high) + dot_nn(latent, low)
    made_ref[i] = (body * scale + total[tokens + channels : tokens + channels + 1]).astype(BF16)

    @pl.when(i == pl.num_programs(0) - 1)
    def _():
        outs = []
        for h in range(made_ref.shape[2] // HEAD):
            cols = slice(h * HEAD, (h + 1) * HEAD)
            scores = dot_nt(made_ref[0, :, cols], made_ref[1, :, cols]) * (math.log2(math.e) / math.sqrt(HEAD))
            weights = jnp.exp2(scores - jnp.max(scores, axis=-1, keepdims=True)).astype(BF16)
            values = made_ref[2, :, cols]
            mixed = dot_nn(weights, jnp.concatenate([values, jnp.ones_like(values)], axis=1))
            outs.append((mixed[:, :HEAD] / mixed[:, HEAD:]).astype(BF16))
        attended = jnp.concatenate(outs, axis=1)
        head_high, head_low = split_two(heads_ref[...] + head_shares(extra_ref))
        result = dot_nt(attended, head_high) + dot_nt(attended, head_low)
        peers, pair_rows, _ = out_ref.shape
        for p in range(peers):
            at = 2 * p * pair_rows
            block = jnp.concatenate([result[at : at + pair_rows], result[at + pair_rows : at + 2 * pair_rows]], axis=1)
            out_ref[p] = block.astype(BF16)


def finish(mine_ref, everyone_ref, both_ref, initial_ref, out_ref):
    mine = mine_ref[0]
    chips, pair_rows, lanes = everyone_ref.shape
    before = both_ref[0] * (mine & 1).astype(F32)
    for chip in range(chips):
        before = before + jnp.where(chip < (mine >> 1), everyone_ref[chip].astype(F32), 0.0)
    out_ref[:pair_rows, :] = initial_ref[:pair_rows, :] + before[:, : lanes // 2]
    out_ref[pair_rows:, :] = initial_ref[pair_rows:, :] + before[:, lanes // 2 :]


def spread_sum(both_ref, out_ref):
    out_ref[...] = jnp.broadcast_to((both_ref[0] + both_ref[1]).astype(BF16)[None], out_ref.shape)


def per_device(
    states, initial, noise_draws, timesteps, context, modulation, out_gate, embed_weight, qkv_weight, out_weight, head_weight
):
    steps, peers = lax.axis_size("tm"), lax.axis_size("seq")
    chips = steps // 2
    mine = lax.axis_index("tm")
    z, core = mine >> 1, mine & 1
    tokens_here, channels = initial.shape
    rows, cols = qkv_weight.shape[1:]
    tokens = tokens_here * peers
    half = tokens + channels + 16
    reach = chips * rows
    extra = channels + 16
    shape = jax.ShapeDtypeStruct
    place = core[None]

    flip = [(i, i ^ 1) for i in range(steps)]
    same_core = [list(range(0, steps, 2)), list(range(1, steps, 2))]
    one = pl.BlockSpec(memory_space=pltpu.VMEM)
    scalar = pl.BlockSpec(memory_space=pltpu.SMEM)
    params = pltpu.CompilerParams(vmem_limit_bytes=LIMIT)

    pair_rows = tokens_here // 2
    payload, gains, sizes, kicks, chunk = pl.pallas_call(
        pack,
        out_shape=(
            shape((peers, tokens_here, reach + 128), BF16),
            shape((pair_rows, 2 * channels), F32),
            shape((pair_rows, 2 * channels), F32),
            shape((pair_rows, 2 * channels), F32),
            shape((3 * rows + extra, cols), jnp.int16),
        ),
        in_specs=[scalar] * 2 + [one] * 8,
        out_specs=[one] * 5,
        compiler_params=params,
        cost_estimate=pl.CostEstimate(flops=30000000, bytes_accessed=5000000, transcendentals=0),
    )(place, timesteps, states[0], noise_draws[0], out_gate, embed_weight, context, qkv_weight, out_weight.T, head_weight)
    gathered = lax.all_to_all(payload, "seq", 0, 0).reshape(tokens, reach + 128)
    chunks = lax.all_gather(chunk, "tm")
    flipped = lax.ppermute(gathered, "tm", flip)

    def fixed(*dims):
        return pl.BlockSpec(dims, lambda i, place: (0,) * len(dims))

    def halved(body, at, more_in, out_shape, out_specs, scratch, flops):
        return pl.pallas_call(
            body,
            out_shape=out_shape,
            grid_spec=pltpu.PrefetchScalarGridSpec(
                num_scalar_prefetch=1,
                grid=(3,),
                in_specs=[
                    fixed(tokens, reach),
                    pl.BlockSpec((channels, reach), lambda i, place: (0, at(place[0]))),
                    pl.BlockSpec((2, reach), lambda i, place: (0, at(place[0]))),
                    pl.BlockSpec((chips, rows, cols), lambda i, place: (at(place[0]), i, 0)),
                    pl.BlockSpec((chips, extra, cols), lambda i, place: (at(place[0]), 3 * rows // extra, 0)),
                ]
                + more_in,
                out_specs=out_specs,
                scratch_shapes=[pltpu.VMEM((half, reach), BF16), pltpu.VMEM((reach, cols), BF16)] + scratch,
            ),
            compiler_params=pltpu.CompilerParams(vmem_limit_bytes=46 * 1024 * 1024),
            cost_estimate=pl.CostEstimate(flops=flops, bytes_accessed=9000000, transcendentals=0),
        )

    by_kind = pl.BlockSpec((half, cols), lambda i, place: (i, 0))
    sums, heads = halved(
        first_half,
        lambda c: c,
        [],
        (shape((3 * half, cols), F32), shape((channels, cols), F32)),
        [by_kind, fixed(channels, cols)],
        [],
        100000000000,
    )(place, gathered, embed_weight, modulation[0], chunks, chunks)
    shares = halved(
        second_half,
        lambda c: 1 - c,
        [by_kind, fixed(channels, cols), pl.BlockSpec((tokens, 128), lambda i, place: (0, reach // 128))],
        shape((peers, pair_rows, 2 * channels), BF16),
        fixed(peers, pair_rows, 2 * channels),
        [pltpu.VMEM((3, tokens, cols), BF16)],
        4000000000,
    )(place, flipped, embed_weight, modulation[0], chunks, chunks, sums, heads, gathered)
    shares = lax.all_to_all(shares, "seq", 0, 0)
    mixed = jnp.sum(shares.astype(F32), axis=0)

    def unpairs(value):
        return jnp.concatenate([value[:, :channels], value[:, channels:]], axis=0)

    velocity_f = gains * mixed
    drift = sizes * velocity_f + kicks
    both = lax.all_gather(drift, "tm", axis_index_groups=[[2 * i, 2 * i + 1] for i in range(chips)])
    spread = pl.pallas_call(
        spread_sum,
        out_shape=shape((chips, pair_rows, 2 * channels), BF16),
        in_specs=[one],
        out_specs=one,
        compiler_params=pltpu.CompilerParams(vmem_limit_bytes=8 * 1024 * 1024),
    )(both)
    everyone = lax.all_to_all(spread, "tm", 0, 0, axis_index_groups=same_core)
    new_states = pl.pallas_call(
        finish,
        out_shape=shape(initial.shape, F32),
        in_specs=[scalar, one, one, one],
        out_specs=one,
        compiler_params=pltpu.CompilerParams(vmem_limit_bytes=8 * 1024 * 1024),
    )(mine[None], everyone, both, initial)
    return (new_states[None], unpairs(velocity_f).astype(BF16)[None])


def solution(mesh):
    in_specs = (
        P("tm", "seq", None),
        P("seq", None),
        P("tm", "seq", None),
        P("tm", None),
        P("seq", None),
        P("tm", None, None),
        P("tm", None),
        P(),
        P(None, "tm", "seq"),
        P("seq", "tm"),
        P(None, "tm"),
    )
    out_specs = (P("tm", "seq", None), P("tm", "seq", None))
    return jax.shard_map(per_device, mesh=mesh, in_specs=in_specs, out_specs=out_specs, check_vma=False)
```
